512 devices in a mesh: tile: 128 (over z, y, core), lvl: 4 (over x).
Axes of the slice: x: 4, y: 4, z: 16, core: 2. Of those that a mesh axis runs over, the one named last changes fastest.
Arguments:
- coefficients: float32 [5, 65536, 512], P(None, 'tile', 'lvl'), may hold values from -0.3 to 2.7, as said below
- level_masks: int32 [512, 4, 6], P('tile', 'lvl'), may hold values 0 or 1
Outputs:
- advanced: float32 [5, 65536, 512], P(None, 'tile', 'lvl')
- tendency: float32 [5, 65536, 512], P(None, 'tile', 'lvl')
The draws below stay inside these ranges and needn't reach their ends.
Inputs may be any that keep to these rules, and one draw needn't show every extreme that they name: Level-0 coefficients hold the field values there: density in 0.9 to 1.1, each momentum within -0.3 to 0.3, energy in 2.3 to 2.7; every other coefficient lies within -0.006 to 0.006. `level_masks`: 1 keeps that detail level of that tile.
All inputs are finite; a program needn't handle non-finite values. No bound on the sum of `level_masks` on one device may be relied on, other than what follows from the above.
Results may differ from the reference program's by a relative error of at most 0.0003.
Values sent between devices are 32-bit elements; how exact they have to be, the bound alone decides.
A program may use at most 64 MiB of HBM per device.

```python
import math
import jax
import jax.numpy as jnp
import numpy as np
from jax import lax

LEVELS = 6
CELL = 128
FIELDS = 5
TILES_X = 512
TILES_Y = 4
NX = 65536
NY = 512


def level_table_drawn(cell_size, levels):
    grades = np.zeros(cell_size, np.int64)
    for position in range(cell_size):
        if position % (cell_size // 2) != 0:
            trailing = (position & -position).bit_length() - 1
            grades[position] = levels - trailing
    return grades


def draw_coefficients(key, part):
    key = jax.random.fold_in(key, 7)
    cell_size = 2 * 2 ** LEVELS
    grades = level_table_drawn(cell_size, LEVELS)
    coarse_cell = (np.maximum(grades[:, None], grades[None, :]) == 0).astype(np.float32)
    coarse = jnp.tile(jnp.asarray(coarse_cell), (TILES_X, TILES_Y))
    noise_key, scale_key = jax.random.split(key)
    values = jax.random.uniform(noise_key, (FIELDS, NX, NY), jnp.float32, -1.0, 1.0)
    ramp = (1.0 + 2.0 * jnp.arange(TILES_X, dtype=jnp.float32) / TILES_X) / 3.0
    factor = jnp.exp(jax.random.uniform(scale_key, (TILES_X, TILES_Y), jnp.float32, math.log(0.5), 0.0)) * ramp[:, None]
    factor = jnp.repeat(jnp.repeat(factor, cell_size, 0), cell_size, 1)
    unit_plane = jnp.ones((NX, NY), jnp.float32)
    spread = jnp.stack([0.1 * unit_plane, 0.3 * factor, 0.3 * factor, 0.3 * factor, 0.2 * unit_plane])
    base = jnp.array([1.0, 0.0, 0.0, 0.0, 2.5], jnp.float32).reshape(5, 1, 1)
    return jnp.where(coarse > 0.5, base + spread * values, 0.006 * values)


def set_ends(result, own_key, least, largest):
    extent = result.shape
    place = [jax.random.randint(jax.random.fold_in(own_key, axis), (), 0, extent[axis]) for axis in range(len(extent))]
    result = result.at[tuple(place)].set(least)
    longest = extent.index(max(extent))
    place[longest] = (place[longest] + 1) % extent[longest]
    return result.at[tuple(place)].set(largest)


def setup_inputs(seed: int = 0) -> dict:
    arg_keys = jax.random.split(jax.random.key(seed), 3)
    coefficients = draw_coefficients(jax.random.fold_in(arg_keys[2], 71), 0)
    level_masks = set_ends((jax.random.randint(arg_keys[1], (TILES_X, TILES_Y, LEVELS), 0, 4) < 3).astype(jnp.int32), jax.random.fold_in(arg_keys[1], 1), 0, 1)
    return {"coefficients": coefficients, "level_masks": level_masks}


gamma_ratio = 1.4
courant = 0.5

def level_table(cell_size, levels):
    grades = np.zeros(cell_size, np.int64)
    for position in range(cell_size):
        if position % (cell_size // 2) != 0:
            trailing = (position & -position).bit_length() - 1
            grades[position] = levels - trailing
    return grades

def lift_tables(cell_size, levels):
    grades = level_table(cell_size, levels)
    synthesis = np.eye(cell_size)
    analysis = np.eye(cell_size)
    for level_now in range(1, levels + 1):
        stride = cell_size // 2 ** (level_now + 1)
        for position in range(cell_size):
            if grades[position] == level_now:
                if position + stride < cell_size:
                    synthesis[position] = synthesis[position] + 0.5 * (synthesis[position - stride] + synthesis[position + stride])
                    analysis[position, position - stride] = -0.5
                    analysis[position, position + stride] = -0.5
                else:
                    synthesis[position] = synthesis[position] + synthesis[position - stride]
                    analysis[position, position - stride] = -1.0
    return (synthesis, analysis)

def level_onehot(cell_size, levels):
    grades = level_table(cell_size, levels)
    joint_grade = np.maximum(grades[:, None], grades[None, :])
    return (joint_grade[None] == np.arange(levels + 1)[:, None, None]).astype(np.float32)

def keep_mask(level_masks, onehot):
    ones_column = jnp.ones(level_masks.shape[:2] + (1,), jnp.float32)
    extended = jnp.concatenate([ones_column, level_masks.astype(jnp.float32)], 2)
    keep_table = jnp.einsum('abl,lij->aibj', extended, onehot)
    return keep_table.reshape(level_masks.shape[0] * onehot.shape[1], level_masks.shape[1] * onehot.shape[2])

def transform(field_block, matrix):
    fields, rows_all, columns = field_block.shape
    cell_size = matrix.shape[0]
    blocks = field_block.reshape(fields, rows_all // cell_size, cell_size, columns // cell_size, cell_size)
    inner_pass = jnp.einsum('ftkbl,jl->ftkbj', blocks, matrix, precision=lax.Precision.HIGHEST)
    outer_pass = jnp.einsum('ik,ftkbj->ftibj', matrix, inner_pass, precision=lax.Precision.HIGHEST)
    return outer_pass.reshape(fields, rows_all, columns)

def primitives(field_state):
    density = field_state[0]
    inverse = 1.0 / density
    velocity_x = field_state[1] * inverse
    velocity_y = field_state[2] * inverse
    velocity_z = field_state[3] * inverse
    kinetic = 0.5 * (field_state[1] * velocity_x + field_state[2] * velocity_y + field_state[3] * velocity_z)
    pressure = (gamma_ratio - 1.0) * (field_state[4] - kinetic)
    return (density, velocity_x, velocity_y, velocity_z, pressure)

def x_flux_of(field_state):
    density, velocity_x, velocity_y, velocity_z, pressure = primitives(field_state)
    return jnp.stack([field_state[1], field_state[1] * velocity_x + pressure, field_state[2] * velocity_x, field_state[3] * velocity_x, (field_state[4] + pressure) * velocity_x])

def y_flux_of(field_state):
    density, velocity_x, velocity_y, velocity_z, pressure = primitives(field_state)
    return jnp.stack([field_state[2], field_state[1] * velocity_y, field_state[2] * velocity_y + pressure, field_state[3] * velocity_y, (field_state[4] + pressure) * velocity_y])

def slope_along(padded, direction, spacing):
    if direction == 1:
        return (padded[:, :-4] - 8.0 * padded[:, 1:-3] + 8.0 * padded[:, 3:-1] - padded[:, 4:]) / (12.0 * spacing)
    return (padded[:, :, :-4] - 8.0 * padded[:, :, 1:-3] + 8.0 * padded[:, :, 3:-1] - padded[:, :, 4:]) / (12.0 * spacing)

def block_tendency(padded, spacing):
    flux_x = x_flux_of(padded[:, :, 2:-2])
    flux_y = y_flux_of(padded[:, 2:-2, :])
    return -(slope_along(flux_x, 1, spacing) + slope_along(flux_y, 2, spacing))

def physical_tendency(field_state, spacing, cell_size):
    padded = jnp.concatenate([field_state[:, -2:], field_state, field_state[:, :2]], 1)
    padded = jnp.concatenate([padded[:, :, -2:], padded, padded[:, :, :2]], 2)
    tiles_along = field_state.shape[1] // cell_size

    def one_tile(tile_index):
        window = lax.dynamic_slice_in_dim(padded, tile_index * cell_size, cell_size + 4, 1)
        return block_tendency(window, spacing)
    stacked = lax.map(one_tile, jnp.arange(tiles_along, dtype=jnp.int32))
    return jnp.transpose(stacked, (1, 0, 2, 3)).reshape(field_state.shape)

def signal_speed(field_state):
    density, velocity_x, velocity_y, velocity_z, pressure = primitives(field_state)
    sound = jnp.sqrt(gamma_ratio * pressure / density)
    return jnp.max(jnp.maximum(jnp.abs(velocity_x), jnp.abs(velocity_y)) + sound)

def reference(coefficients, level_masks):
    cell_size = CELL
    synthesis, analysis = lift_tables(cell_size, LEVELS)
    synthesis = jnp.asarray(synthesis, jnp.float32)
    analysis = jnp.asarray(analysis, jnp.float32)
    onehot = jnp.asarray(level_onehot(cell_size, LEVELS), jnp.float32)
    keep_table = keep_mask(level_masks, onehot)
    spacing = 1.0 / cell_size
    masked_start = coefficients * keep_table
    state_zero = transform(masked_start, synthesis)
    time_step = courant * spacing / signal_speed(state_zero)
    rate_zero = keep_table * transform(physical_tendency(state_zero, spacing, cell_size), analysis)
    section_one = masked_start + time_step * rate_zero
    state_one = transform(section_one, synthesis)
    rate_one = keep_table * transform(physical_tendency(state_one, spacing, cell_size), analysis)
    rate_total = 0.5 * (rate_zero + rate_one)
    return (masked_start + time_step * rate_total, rate_total)
```

```python
import functools

import jax
import jax.numpy as jnp
from jax import lax
from jax.experimental import pallas as pl
from jax.experimental.pallas import tpu as pltpu
from jax.sharding import PartitionSpec as P

MESH = pl.DeviceIdType.MESH
F32 = jnp.float32
BF16 = jnp.bfloat16
FIELDS = 5
CELL = 128
SEG = 64
ROWS = 512
BASE_DENSITY = 1.0
BASE_ENERGY = 2.5
SPACING = 1.0 / CELL


def iota(shape, axis):
    return lax.broadcasted_iota(jnp.int32, shape, axis)


def stride_of(position):
    low = jnp.bitwise_and(position, -position)
    return jnp.where(jnp.bitwise_and(position, 63) == 0, 64, low)


def level_of(stride):
    level = jnp.zeros_like(stride)
    for number in range(1, 7):
        level = jnp.where(stride == 64 >> number, number, level)
    return level


def synthesis_t():
    q, p = iota((CELL, CELL), 0), iota((CELL, CELL), 1)
    s = stride_of(q)
    hat = jnp.maximum(1.0 - jnp.abs(p - q).astype(F32) / s.astype(F32), 0.0)
    return jnp.where(jnp.logical_and(q + s == CELL, p >= q), 1.0, hat)


def analysis_t():
    q, p = iota((CELL, CELL), 0), iota((CELL, CELL), 1)
    s = stride_of(p)
    detail = jnp.bitwise_and(p, 63) != 0
    last = p + s == CELL
    left = jnp.where(jnp.logical_and(detail, q == p - s), jnp.where(last, 1.0, 0.5), 0.0)
    right = jnp.where(
        jnp.logical_and(detail, jnp.logical_and(jnp.logical_not(last), q == p + s)), 0.5, 0.0
    )
    return jnp.where(p == q, 1.0, 0.0) - left - right


def slope_matrix(j, i):
    d = j - i
    near = jnp.where(d == 1, 8.0, 0.0) - jnp.where(d == -1, 8.0, 0.0)
    return near + jnp.where(d == -2, 1.0, 0.0) - jnp.where(d == 2, 1.0, 0.0)


def halo_point(slot):
    return jnp.where(slot < 2, slot - 2, slot + 126)


def dot(a, b):
    return lax.dot_general(a, b, (((1,), (0,)), ((), ())), preferred_element_type=F32)


def halves(x):
    high = x.astype(BF16)
    return high, (x - high.astype(F32)).astype(BF16)


def neighbours(nodes, even):
    following = pltpu.roll(nodes[0], 7, 0)
    end = jnp.where(even, following, nodes[-1])[None]
    return end if nodes.shape[0] == 1 else jnp.concatenate([nodes[1:], end], 0)


def row_synthesis(c, even):
    nodes = c[0:1]
    s = SEG // 2
    while s >= 1:
        count = SEG // (2 * s)
        detail = c.reshape(count, 2 * s, 8, CELL)[:, s]
        middle = detail + 0.5 * (nodes + neighbours(nodes, even))
        nodes = jnp.stack([nodes, middle], 1).reshape(2 * count, 8, CELL)
        s //= 2
    return nodes


def row_analysis(u, even):
    pieces = u[0:1]
    s = SEG // 2
    while s >= 1:
        count = SEG // (2 * s)
        both = u.reshape(count, 2, s, 8, CELL)
        left, middle = both[:, 0, 0], both[:, 1, 0]
        detail = middle - 0.5 * (left + neighbours(left, even))
        pieces = jnp.stack([pieces, detail], 1).reshape(2 * count, 8, CELL)
        s //= 2
    return pieces


def row_level(p):
    return 0 if p == 0 else 6 - ((p & -p).bit_length() - 1)


def primitives(q):
    inverse = 1.0 / q[0]
    vx, vy, vz = q[1] * inverse, q[2] * inverse, q[3] * inverse
    xx, yy, zz = q[1] * vx, q[2] * vy, q[3] * vz
    excess = 0.4 * ((q[4] - BASE_ENERGY) - 0.5 * (xx + yy + zz))
    return inverse, vx, vy, xx, yy, excess


def x_flux(q, prim):
    _, vx, _, xx, _, excess = prim
    enthalpy = q[4] + excess + 0.4 * BASE_ENERGY
    return [q[1], xx + excess, q[2] * vx, q[3] * vx, enthalpy * vx]


def y_flux(q, prim):
    _, _, vy, _, yy, excess = prim
    enthalpy = q[4] + excess + 0.4 * BASE_ENERGY
    return [q[2], q[1] * vy, yy + excess, q[3] * vy, enthalpy * vy]


def speed(prim):
    inverse, vx, vy, _, _, excess = prim
    sound = jnp.sqrt(1.4 * (excess + 0.4 * BASE_ENERGY) * inverse)
    return jnp.maximum(jnp.abs(vx), jnp.abs(vy)) + sound


def pack_edges(u, lane):
    def gather(part):
        width = 64
        while part.shape[0] > 1:
            n = part.shape[0] // 2
            chosen = jnp.bitwise_and(lane + 2, width) != 0
            part = jnp.where(chosen, pltpu.roll(part[n:], width, 2), part[:n])
            width //= 2
        return part[0]

    first, second = gather(u[:32]), pltpu.roll(gather(u[32:]), 2, 1)
    upper = jnp.bitwise_and(lane, 3) >= 2
    return jnp.where(upper, first, second), jnp.where(upper, second, first)


CHUNK = 4


def kernel(
    n_tile, n_lvl, inner,
    coef, masks, adv, ten,
    cin, oadv, oten, st, rr, fx, fy, rate0, wmat, hmask, mk,
    row_snd, row_rcv, col_snd, col_rcv, mx_snd, mx_rcv,
    in_sem, out_sem, row_ss, row_rs, col_ss, col_rs, mx_ss, mx_rs,
):
    outer = n_tile // inner
    tile, lvl = lax.axis_index("tile"), lax.axis_index("lvl")
    z, low = tile // inner, tile % inner
    t_right, t_left = lax.rem(tile + 1, n_tile), lax.rem(tile + n_tile - 1, n_tile)
    l_right, l_left = lax.rem(lvl + 1, n_lvl), lax.rem(lvl + n_lvl - 1, n_lvl)

    load = [
        pltpu.make_async_copy(coef.at[f], cin.at[pl.ds(f * ROWS, ROWS)], in_sem.at[f])
        for f in range(FIELDS)
    ]
    for copy in load:
        copy.start()

    groups = [
        [(tile, lax.rem(lvl + k, n_lvl)) for k in range(1, n_lvl)],
        [(z * inner + lax.rem(low + k, inner), lvl) for k in range(1, inner)],
        [(lax.rem(z + k, outer) * inner + low, lvl) for k in range(1, outer)],
    ]
    barrier = pltpu.get_barrier_semaphore()
    partners = [(t_right, lvl), (t_left, lvl), (tile, l_right), (tile, l_left)]
    partners += groups[0] + groups[1] + groups[2]
    for partner in partners:
        pl.semaphore_signal(barrier, inc=1, device_id=partner, device_id_type=MESH)

    sub, lane = iota((8, CELL), 0), iota((8, CELL), 1)
    even = jnp.bitwise_and(sub, 1) == 0

    synth = synthesis_t().astype(BF16)
    at = analysis_t().astype(BF16)
    k, i = iota((CELL, CELL), 0), iota((CELL, CELL), 1)
    wmat[0, :CELL], wmat[0, CELL:] = synth, synth
    wmat[1, :CELL] = at
    wmat[1, CELL:] = dot(slope_matrix(k, i).astype(BF16), at).astype(BF16)
    for part, offset in ((2, 2), (3, 0)):
        edge = slope_matrix(halo_point(jnp.bitwise_and(k + offset, 3)), i).astype(BF16)
        edge = dot(edge, at).astype(BF16)
        wmat[part, :CELL], wmat[part, CELL:] = edge, edge
    row, col = iota((32 * 8, CELL), 0), iota((32 * 8, CELL), 1)
    for part, offset in ((0, 2), (1, 0)):
        group = jnp.right_shift(jnp.bitwise_and(col + offset, 127), 2)
        hmask[part] = jnp.where(group == jnp.right_shift(row, 3), 1.0, 0.0).astype(BF16)

    level = level_of(stride_of(lane))
    owner = jnp.right_shift(sub, 1)
    planes = [jnp.ones((8, CELL), F32)]
    for number in range(6):
        plane = jnp.full((8, CELL), masks[0, 0, number], jnp.int32)
        for t in range(1, 4):
            plane = jnp.where(owner == t, masks[t, 0, number], plane)
        planes.append(plane.astype(F32))
    for number in range(7):
        keep = planes[number]
        for other in range(number + 1, 7):
            keep = jnp.where(level == other, planes[other], keep)
        mk[number] = keep

    def by_level(scale=None):
        keeps = [mk[number] if scale is None else mk[number] * scale for number in range(7)]
        return lambda p: keeps[row_level(p)]

    def start_of(f, keep_at):
        return [
            cin[pl.ds(f * ROWS + p, 8, SEG), :] * keep_at(p) for p in range(SEG)
        ]

    def base_of(f):
        return jnp.where(f == 0, BASE_DENSITY, jnp.where(f == 4, BASE_ENERGY, 0.0)).astype(F32)

    def synthesise(c):
        high, low_part = halves(c.reshape(ROWS, CELL))
        out = dot(jnp.concatenate([high, low_part], 1), wmat[0])
        return row_synthesis(out.reshape(SEG, 8, CELL), even)

    def send_edges(stage, f, u):
        to_right, to_left = pack_edges(u, lane)
        col_snd[stage, 0, f] = to_right
        col_snd[stage, 1, f] = to_left
        for r in range(2):
            row_snd[stage, 0, pl.ds(2 * f + r, 1), :] = u[62 + r, 7:8]
            row_snd[stage, 1, pl.ds(2 * f + r, 1), :] = u[r, 0:1]

    def edge_copies(stage):
        copies = []
        for side, (t_to, l_to) in enumerate(((t_right, l_right), (t_left, l_left))):
            copies.append(pltpu.make_async_remote_copy(
                col_snd.at[stage, side], col_rcv.at[stage, side],
                col_ss.at[stage, side], col_rs.at[stage, side],
                device_id=(tile, l_to), device_id_type=MESH))
            copies.append(pltpu.make_async_remote_copy(
                row_snd.at[stage, side], row_rcv.at[stage, side],
                row_ss.at[stage, side], row_rs.at[stage, side],
                device_id=(t_to, lvl), device_id_type=MESH))
        return copies

    for copy in load:
        copy.wait()

    def first(f, _):
        base = base_of(f)
        parts = start_of(f, by_level())
        parts[0] = parts[0] - jnp.where(jnp.bitwise_and(lane, 63) == 0, base, 0.0)
        u = synthesise(jnp.stack(parts, 0)) + base
        st[f] = u
        send_edges(0, f, u)
        return 0

    lax.fori_loop(0, FIELDS, first, 0)
    pl.semaphore_wait(barrier, len(partners))
    edges = [edge_copies(0), edge_copies(1)]
    for copy in edges[0]:
        copy.start()

    def fluxes(stage, dt):
        def chunk(c, top):
            at_rows = pl.ds(c * CHUNK, CHUNK)
            q = [st[f, at_rows] for f in range(FIELDS)]
            if stage:
                q = [q[f] + dt * rr[f, at_rows] for f in range(FIELDS)]
            prim = primitives(q)
            for f, value in enumerate(x_flux(q, prim)):
                fx[f, pl.ds(c * CHUNK + 2, CHUNK)] = value
            for f, value in enumerate(y_flux(q, prim)):
                fy[f, at_rows] = value
            if stage == 0:
                top = jnp.maximum(top, jnp.max(speed(prim), 0))
            return top

        return lax.fori_loop(0, SEG // CHUNK, chunk, jnp.zeros((8, CELL), F32))

    def rounds(number):
        copies = []
        for slot, partner in enumerate(groups[number]):
            copies.append(pltpu.make_async_remote_copy(
                mx_snd.at[number], mx_rcv.at[number, slot],
                mx_ss.at[number], mx_rs.at[number],
                device_id=partner, device_id_type=MESH))
        return copies

    def send_top(number, top):
        mx_snd[number] = top
        for copy in rounds(number):
            copy.start()

    def take_top(number, top):
        count = len(groups[number])
        whole = mx_rcv.at[number, pl.ds(0, count)]
        pltpu.make_async_copy(whole, whole, mx_rs.at[number]).wait()
        return jnp.maximum(top, jnp.max(mx_rcv[number, 0:count], 0))

    def ext_rows(stage, f, side, r, dt):
        source = st[f, 62 + r] if side == 0 else st[f, r]
        beyond = row_rcv[0, side, pl.ds(2 * f + r, 1), :]
        if stage:
            source = source + dt * (rr[f, 62 + r] if side == 0 else rr[f, r])
            beyond = beyond + dt[0:1] * row_rcv[1, side, pl.ds(2 * f + r, 1), :]
        rolled = pltpu.roll(source, 1 if side == 0 else 7, 0)
        return jnp.where(sub == (0 if side == 0 else 7), beyond, rolled)

    upper = jnp.bitwise_and(lane, 3) >= 2

    def halo_fluxes(stage, dt):
        q = [
            jnp.stack([ext_rows(stage, f, side, r, dt) for side in range(2) for r in range(2)], 0)
            for f in range(FIELDS)
        ]
        for f, value in enumerate(x_flux(q, primitives(q))):
            fx[f, 0:2] = value[0:2]
            fx[f, SEG + 2:SEG + 4] = value[2:4]
        q = []
        for f in range(FIELDS):
            from_left, from_right = col_rcv[0, 0, f], col_rcv[0, 1, f]
            if stage:
                from_left = from_left + dt * col_rcv[1, 0, f]
                from_right = from_right + dt * col_rcv[1, 1, f]
            q.append(jnp.stack([
                jnp.where(upper, from_left, from_right), jnp.where(upper, from_right, from_left)
            ], 0))
        return y_flux(q, primitives(q))

    def analysed(f, edge):
        g = fx[f]
        slope = 8.0 * (g[3:67] - g[1:65]) - (g[4:68] - g[0:64])
        xh, xl = halves(slope.reshape(ROWS, CELL))
        yh, yl = halves(fy[f].reshape(ROWS, CELL))
        weights = wmat[1]
        out = dot(jnp.concatenate([xh, yh], 1), weights) + dot(jnp.concatenate([xl, yl], 1), weights)
        extra = []
        for part in range(2):
            eh, el = halves(jnp.concatenate([edge[part], edge[part]], 0))
            spread = hmask[part]
            eh = jnp.concatenate([eh] * 16, 0) * spread
            el = jnp.concatenate([el] * 16, 0) * spread
            extra.append(dot(jnp.concatenate([eh, el], 1), wmat[2 + part]))
        out = out + jnp.concatenate(extra, 0)
        return row_analysis(out.reshape(SEG, 8, CELL), even)

    zero = jnp.zeros((8, CELL), F32)
    top = jnp.max(fluxes(0, zero), 0, keepdims=True)
    send_top(0, top)
    for copy in edges[0]:
        copy.wait_recv()
    top = take_top(0, top)
    send_top(1, top)
    edge_flux = halo_fluxes(0, zero)
    scale = -1.0 / (12.0 * SPACING)
    for f in range(FIELDS):
        keep_at = by_level(scale)
        d = analysed(f, edge_flux[f])
        rate = jnp.stack([d[p] * keep_at(p) for p in range(SEG)], 0)
        rate0[f] = rate
        u = synthesise(rate)
        rr[f] = u
        send_edges(1, f, u)
        if f == 2:
            top = take_top(1, top)
            send_top(2, top)
    for copy in edges[1]:
        copy.start()
    top = take_top(2, top)
    top = jnp.max(top, 1, keepdims=True)
    dt = 0.5 * SPACING / jnp.broadcast_to(top, (8, CELL))
    fluxes(1, dt)
    for copy in edges[1]:
        copy.wait_recv()
    edge_flux = halo_fluxes(1, dt)
    store = []
    for f in range(FIELDS):
        keep_at = by_level(0.5 * scale)
        d = analysed(f, edge_flux[f])
        for p in range(SEG):
            value = 0.5 * rate0[f, p] + d[p] * keep_at(p)
            rows = pl.ds(f * ROWS + p, 8, SEG)
            start = cin[rows, :] * mk[row_level(p)]
            oten[rows, :] = value
            oadv[rows, :] = start + dt * value
        for number, (source, target) in enumerate(((oadv, adv), (oten, ten))):
            copy = pltpu.make_async_copy(
                source.at[pl.ds(f * ROWS, ROWS)], target.at[f], out_sem.at[number, f])
            copy.start()
            store.append(copy)
    for copy in edges[0] + edges[1]:
        copy.wait_send()
    for number in range(3):
        for copy in rounds(number):
            copy.wait_send()
    for copy in store:
        copy.wait()


def solution(mesh):
    n_tile, n_lvl = mesh.shape["tile"], mesh.shape["lvl"]
    inner = 8 if n_tile > 8 and n_tile % 8 == 0 else 2
    most = max(n_lvl, inner, n_tile // inner) - 1
    block = (FIELDS, SEG, 8, CELL)
    flat = (FIELDS * ROWS, CELL)
    dma = pltpu.SemaphoreType.DMA

    def shards(coefficients, level_masks):
        result = jax.ShapeDtypeStruct((FIELDS, ROWS, CELL), F32)
        return pl.pallas_call(
            functools.partial(kernel, n_tile, n_lvl, inner),
            out_shape=(result, result),
            in_specs=[
                pl.BlockSpec(memory_space=pl.ANY),
                pl.BlockSpec(memory_space=pltpu.SMEM),
            ],
            out_specs=(pl.BlockSpec(memory_space=pl.ANY), pl.BlockSpec(memory_space=pl.ANY)),
            scratch_shapes=[
                pltpu.VMEM(flat, F32), pltpu.VMEM(flat, F32), pltpu.VMEM(flat, F32),
                pltpu.VMEM(block, F32), pltpu.VMEM(block, F32),
                pltpu.VMEM((FIELDS, SEG + 4, 8, CELL), F32), pltpu.VMEM(block, F32),
                pltpu.VMEM(block, F32),
                pltpu.VMEM((4, 2 * CELL, CELL), BF16), pltpu.VMEM((2, 256, CELL), BF16),
                pltpu.VMEM((7, 8, CELL), F32),
                pltpu.VMEM((2, 2, 16, CELL), F32), pltpu.VMEM((2, 2, 16, CELL), F32),
                pltpu.VMEM((2, 2, FIELDS, 8, CELL), F32), pltpu.VMEM((2, 2, FIELDS, 8, CELL), F32),
                pltpu.VMEM((3, 1, CELL), F32), pltpu.VMEM((3, most, 1, CELL), F32),
                dma((FIELDS,)), dma((2, FIELDS)),
                dma((2, 2)), dma((2, 2)), dma((2, 2)), dma((2, 2)), dma((3,)), dma((3,)),
            ],
            compiler_params=pltpu.CompilerParams(
                collective_id=0, has_side_effects=True, vmem_limit_bytes=40 * 2**20
            ),
        )(coefficients, level_masks)

    specs = P(None, "tile", "lvl")
    return jax.shard_map(
        shards, mesh=mesh, in_specs=(specs, P("tile", "lvl", None)), out_specs=(specs, specs),
        check_vma=False,
    )
```

```python
import functools

import jax
import jax.numpy as jnp
from jax import lax
from jax.experimental import pallas as pl
from jax.experimental.pallas import tpu as pltpu
from jax.sharding import PartitionSpec as P

MESH = pl.DeviceIdType.MESH
F32 = jnp.float32
BF16 = jnp.bfloat16
FIELDS = 5
CELL = 128
SEG = 64
ROWS = 512
BASE_DENSITY = 1.0
BASE_ENERGY = 2.5
SPACING = 1.0 / CELL


def iota(shape, axis):
    return lax.broadcasted_iota(jnp.int32, shape, axis)


def stride_of(position):
    low = jnp.bitwise_and(position, -position)
    return jnp.where(jnp.bitwise_and(position, 63) == 0, 64, low)


def level_of(stride):
    level = jnp.zeros_like(stride)
    for number in range(1, 7):
        level = jnp.where(stride == 64 >> number, number, level)
    return level


def synthesis_t():
    q, p = iota((CELL, CELL), 0), iota((CELL, CELL), 1)
    s = stride_of(q)
    hat = jnp.maximum(1.0 - jnp.abs(p - q).astype(F32) / s.astype(F32), 0.0)
    return jnp.where(jnp.logical_and(q + s == CELL, p >= q), 1.0, hat)


def analysis_t():
    q, p = iota((CELL, CELL), 0), iota((CELL, CELL), 1)
    s = stride_of(p)
    detail = jnp.bitwise_and(p, 63) != 0
    last = p + s == CELL
    left = jnp.where(jnp.logical_and(detail, q == p - s), jnp.where(last, 1.0, 0.5), 0.0)
    right = jnp.where(
        jnp.logical_and(detail, jnp.logical_and(jnp.logical_not(last), q == p + s)), 0.5, 0.0
    )
    return jnp.where(p == q, 1.0, 0.0) - left - right


def slope_matrix(j, i):
    d = j - i
    near = jnp.where(d == 1, 8.0, 0.0) - jnp.where(d == -1, 8.0, 0.0)
    return near + jnp.where(d == -2, 1.0, 0.0) - jnp.where(d == 2, 1.0, 0.0)


def halo_point(slot):
    return jnp.where(slot < 2, slot - 2, slot + 126)


def dot(a, b):
    return lax.dot_general(a, b, (((1,), (0,)), ((), ())), preferred_element_type=F32)


def halves(x):
    high = x.astype(BF16)
    return high, (x - high.astype(F32)).astype(BF16)


def neighbours(nodes, even):
    following = pltpu.roll(nodes[0], 7, 0)
    end = jnp.where(even, following, nodes[-1])[None]
    return end if nodes.shape[0] == 1 else jnp.concatenate([nodes[1:], end], 0)


def row_synthesis(c, even):
    nodes = c[0:1]
    s = SEG // 2
    while s >= 1:
        count = SEG // (2 * s)
        detail = c.reshape(count, 2 * s, 8, CELL)[:, s]
        middle = detail + 0.5 * (nodes + neighbours(nodes, even))
        nodes = jnp.stack([nodes, middle], 1).reshape(2 * count, 8, CELL)
        s //= 2
    return nodes


def row_analysis(u, even):
    pieces = u[0:1]
    s = SEG // 2
    while s >= 1:
        count = SEG // (2 * s)
        both = u.reshape(count, 2, s, 8, CELL)
        left, middle = both[:, 0, 0], both[:, 1, 0]
        detail = middle - 0.5 * (left + neighbours(left, even))
        pieces = jnp.stack([pieces, detail], 1).reshape(2 * count, 8, CELL)
        s //= 2
    return pieces


def row_level(p):
    return 0 if p == 0 else 6 - ((p & -p).bit_length() - 1)


def primitives(q):
    inverse = 1.0 / q[0]
    vx, vy, vz = q[1] * inverse, q[2] * inverse, q[3] * inverse
    xx, yy, zz = q[1] * vx, q[2] * vy, q[3] * vz
    excess = 0.4 * ((q[4] - BASE_ENERGY) - 0.5 * (xx + yy + zz))
    return inverse, vx, vy, xx, yy, excess


def x_flux(q, prim):
    _, vx, _, xx, _, excess = prim
    enthalpy = q[4] + excess + 0.4 * BASE_ENERGY
    return [q[1], xx + excess, q[2] * vx, q[3] * vx, enthalpy * vx]


def y_flux(q, prim):
    _, _, vy, _, yy, excess = prim
    enthalpy = q[4] + excess + 0.4 * BASE_ENERGY
    return [q[2], q[1] * vy, yy + excess, q[3] * vy, enthalpy * vy]


def speed(prim):
    inverse, vx, vy, _, _, excess = prim
    sound = jnp.sqrt(1.4 * (excess + 0.4 * BASE_ENERGY) * inverse)
    return jnp.maximum(jnp.abs(vx), jnp.abs(vy)) + sound


def pack_edges(u, lane):
    def gather(part):
        width = 64
        while part.shape[0] > 1:
            n = part.shape[0] // 2
            chosen = jnp.bitwise_and(lane + 2, width) != 0
            part = jnp.where(chosen, pltpu.roll(part[n:], width, 2), part[:n])
            width //= 2
        return part[0]

    first, second = gather(u[:32]), pltpu.roll(gather(u[32:]), 2, 1)
    upper = jnp.bitwise_and(lane, 3) >= 2
    return jnp.where(upper, first, second), jnp.where(upper, second, first)


CHUNK = 4
EXT = SEG + 4


def flux_pass(state_at, fx, fy):
    def chunk(c, _):
        rows = pl.ds(c * CHUNK, CHUNK)
        q = state_at(rows)
        prim = primitives(q)
        for f, value in enumerate(x_flux(q, prim)):
            fx[f, rows] = value
        for f, value in enumerate(y_flux(q, prim)):
            fy[f, rows] = value
        return 0

    lax.fori_loop(0, EXT // CHUNK, chunk, 0)


def analysed(f, edge, fx, fy, wmat, hmask, even):
    g = fx[f]
    slope = 8.0 * (g[3:67] - g[1:65]) - (g[4:68] - g[0:64])
    xh, xl = halves(slope.reshape(ROWS, CELL))
    yh, yl = halves(fy[f, 2:66].reshape(ROWS, CELL))
    weights = wmat[1]
    out = dot(jnp.concatenate([xh, yh], 1), weights) + dot(jnp.concatenate([xl, yl], 1), weights)
    extra = []
    for part in range(2):
        eh, el = halves(jnp.concatenate([edge[part], edge[part]], 0))
        spread = hmask[part]
        eh = jnp.concatenate([eh] * 16, 0) * spread
        el = jnp.concatenate([el] * 16, 0) * spread
        extra.append(dot(jnp.concatenate([eh, el], 1), wmat[2 + part]))
    out = out + jnp.concatenate(extra, 0)
    return row_analysis(out.reshape(SEG, 8, CELL), even)


def build_weights(wmat, hmask):
    synth = synthesis_t().astype(BF16)
    at = analysis_t().astype(BF16)
    k, i = iota((CELL, CELL), 0), iota((CELL, CELL), 1)
    wmat[0, :CELL], wmat[0, CELL:] = synth, synth
    wmat[1, :CELL] = at
    wmat[1, CELL:] = dot(slope_matrix(k, i).astype(BF16), at).astype(BF16)
    for part, offset in ((2, 2), (3, 0)):
        edge = slope_matrix(halo_point(jnp.bitwise_and(k + offset, 3)), i).astype(BF16)
        edge = dot(edge, at).astype(BF16)
        wmat[part, :CELL], wmat[part, CELL:] = edge, edge
    row, col = iota((32 * 8, CELL), 0), iota((32 * 8, CELL), 1)
    for part, offset in ((0, 2), (1, 0)):
        group = jnp.right_shift(jnp.bitwise_and(col + offset, 127), 2)
        hmask[part] = jnp.where(group == jnp.right_shift(row, 3), 1.0, 0.0).astype(BF16)


def build_keep(masks, mk, mkd, sub, lane):
    level = level_of(stride_of(lane))
    owner = jnp.right_shift(sub, 1)
    planes = [jnp.ones((8, CELL), F32)]
    for number in range(6):
        plane = jnp.full((8, CELL), masks[0, 0, number], jnp.int32)
        for t in range(1, 4):
            plane = jnp.where(owner == t, masks[t, 0, number], plane)
        planes.append(plane.astype(F32))
    for number in range(7):
        keep = planes[number]
        for other in range(number + 1, 7):
            keep = jnp.where(level == other, planes[other], keep)
        mk[number] = keep
        mkd[number] = keep * (-0.5 / (12.0 * SPACING))


def front(
    n_tile, n_lvl, inner, reach,
    coef, masks,
    start, half0, st, rr, cols, dts, wmat, hmask, mkd,
    cin, lvm, fx, fy, mk,
    row_snd, row_rcv, col_snd, col_rcv, mx_snd, mx_rcv,
    in_sem, mask_sem, row_ss, row_rs, col_ss, col_rs, mx_ss, mx_rs,
):
    outer = n_tile // inner
    tile, lvl = lax.axis_index("tile"), lax.axis_index("lvl")
    z, low = tile // inner, tile % inner
    t_right, t_left = lax.rem(tile + 1, n_tile), lax.rem(tile + n_tile - 1, n_tile)
    l_right, l_left = lax.rem(lvl + 1, n_lvl), lax.rem(lvl + n_lvl - 1, n_lvl)

    load_masks = pltpu.make_async_copy(masks, lvm, mask_sem)
    load_masks.start()
    load = [
        pltpu.make_async_copy(coef.at[f], cin.at[pl.ds(f * ROWS, ROWS)], in_sem.at[f])
        for f in range(FIELDS)
    ]
    for copy in load:
        copy.start()

    def there(dz, dlow, dx):
        to = lax.rem(z + outer + dz, outer) * inner + lax.rem(low + dlow, inner)
        return to, lax.rem(lvl + dx, n_lvl)

    spread = sorted(range(-reach, reach + 1), key=lambda d: -abs(d))
    jumps = sorted({d % outer for d in (-reach, 0, reach)}, key=lambda d: d == 0)
    spread = list(dict.fromkeys(d % outer for d in spread))
    groups = [
        [there(dz, 0, dx) for dz in spread for dx in range(n_lvl) if dz or dx],
        [there(dz, dlow, 0) for dz in jumps for dlow in range(inner) if dz or dlow],
    ]
    partners = groups[0] + groups[1]
    partners += [(t_right, lvl), (t_left, lvl), (tile, l_right), (tile, l_left)]
    barrier = pltpu.get_barrier_semaphore()
    for partner in partners:
        pl.semaphore_signal(barrier, inc=1, device_id=partner, device_id_type=MESH)

    sub, lane = iota((8, CELL), 0), iota((8, CELL), 1)
    even = jnp.bitwise_and(sub, 1) == 0
    upper = jnp.bitwise_and(lane, 3) >= 2
    coarse = jnp.bitwise_and(lane, 63) == 0
    build_weights(wmat, hmask)
    load_masks.wait()
    build_keep(lvm, mk, mkd, sub, lane)

    def synthesise(c):
        high, low_part = halves(c.reshape(ROWS, CELL))
        out = dot(jnp.concatenate([high, low_part], 1), wmat[0])
        return row_synthesis(out.reshape(SEG, 8, CELL), even)

    def pack(stage, f, u):
        to_right, to_left = pack_edges(u, lane)
        col_snd[stage, 0, f] = to_right
        col_snd[stage, 1, f] = to_left
        for r in range(2):
            row_snd[stage, 0, pl.ds(2 * f + r, 1), :] = u[62 + r, 7:8]
            row_snd[stage, 1, pl.ds(2 * f + r, 1), :] = u[r, 0:1]

    def edge_copies(stage):
        copies = []
        for side, (t_to, l_to) in enumerate(((t_right, l_right), (t_left, l_left))):
            copies.append(pltpu.make_async_remote_copy(
                col_snd.at[stage, side], col_rcv.at[stage, side],
                col_ss.at[stage, side], col_rs.at[stage, side],
                device_id=(tile, l_to), device_id_type=MESH))
            copies.append(pltpu.make_async_remote_copy(
                row_snd.at[stage, side], row_rcv.at[stage, side],
                row_ss.at[stage, side], row_rs.at[stage, side],
                device_id=(t_to, lvl), device_id_type=MESH))
        return copies

    def rounds(number):
        return [
            pltpu.make_async_remote_copy(
                mx_snd.at[number], mx_rcv.at[number, slot], mx_ss.at[number], mx_rs.at[number],
                device_id=partner, device_id_type=MESH)
            for slot, partner in enumerate(groups[number])
        ]

    def take_top(number, top):
        count = len(groups[number])
        whole = mx_rcv.at[number, pl.ds(0, count)]
        pltpu.make_async_copy(whole, whole, mx_rs.at[number]).wait()
        return jnp.maximum(top, jnp.max(mx_rcv[number, 0:count], 0))

    def take_edges(stage, block):
        for f in range(FIELDS):
            for side in range(2):
                for r in range(2):
                    source = block[f, 64 + r] if side == 0 else block[f, 2 + r]
                    beyond = row_rcv[stage, side, pl.ds(2 * f + r, 1), :]
                    rolled = pltpu.roll(source, 1 if side == 0 else 7, 0)
                    here = r if side == 0 else 66 + r
                    block[f, here] = jnp.where(sub == (0 if side == 0 else 7), beyond, rolled)
            from_left, from_right = col_rcv[stage, 0, f], col_rcv[stage, 1, f]
            cols[stage, f, 0] = jnp.where(upper, from_left, from_right)
            cols[stage, f, 1] = jnp.where(upper, from_right, from_left)

    for f in range(FIELDS):
        load[f].wait()
        parts = [cin[pl.ds(f * ROWS + p, 8, SEG), :] * mk[row_level(p)] for p in range(SEG)]
        parts = jnp.stack(parts, 0)
        start[f] = parts
        base = {0: BASE_DENSITY, 4: BASE_ENERGY}.get(f)
        if base:
            first = jnp.where(coarse, parts[0:1] - base, parts[0:1])
            parts = jnp.concatenate([first, parts[1:]], 0)
        u = synthesise(parts)
        if base:
            u = u + base
        st[f, 2:66] = u
        pack(0, f, u)

    def fastest(c, top):
        rows = pl.ds(c * CHUNK + 2, CHUNK)
        prim = primitives([st[f, rows] for f in range(FIELDS)])
        return jnp.maximum(top, jnp.max(speed(prim), 0))

    top = lax.fori_loop(0, SEG // CHUNK, fastest, jnp.zeros((8, CELL), F32))
    top = jnp.max(top, 0, keepdims=True)
    mx_snd[0] = top
    pl.semaphore_wait(barrier, len(partners))
    first_round, second_round = rounds(0), rounds(1)
    edges = [edge_copies(0), edge_copies(1)]
    for copy in first_round + edges[0]:
        copy.start()

    for copy in edges[0]:
        copy.wait_recv()
    take_edges(0, st)
    flux_pass(lambda rows: [st[f, rows] for f in range(FIELDS)], fx, fy)
    q = [cols[0, f] for f in range(FIELDS)]
    edge_flux = y_flux(q, primitives(q))
    for f in range(FIELDS):
        d = analysed(f, edge_flux[f], fx, fy, wmat, hmask, even)
        half = jnp.stack([d[p] * mkd[row_level(p)] for p in range(SEG)], 0)
        half0[f] = half
        u = synthesise(half + half)
        rr[f, 2:66] = u
        pack(1, f, u)
    for copy in edges[1]:
        copy.start()
    top = take_top(0, top)
    mx_snd[1] = top
    for copy in second_round:
        copy.start()
    for copy in edges[1]:
        copy.wait_recv()
    take_edges(1, rr)
    for copy in edges[0] + edges[1] + first_round:
        copy.wait_send()
    top = take_top(1, top)
    top = jnp.max(top, 1, keepdims=True)
    dts[...] = 0.5 * SPACING / jnp.broadcast_to(top, (8, CELL))
    for copy in second_round:
        copy.wait_send()


def back(
    start, half0, st, rr, cols, dts, wmat, hmask, mkd, adv, ten, oadv, oten, fx, fy, out_sem
):
    even = jnp.bitwise_and(iota((8, CELL), 0), 1) == 0
    dt = dts[...]
    flux_pass(lambda rows: [st[f, rows] + dt * rr[f, rows] for f in range(FIELDS)], fx, fy)
    q = [cols[0, f] + dt * cols[1, f] for f in range(FIELDS)]
    edge_flux = y_flux(q, primitives(q))
    store = []
    for f in range(FIELDS):
        d = analysed(f, edge_flux[f], fx, fy, wmat, hmask, even)
        for p in range(SEG):
            value = half0[f, p] + d[p] * mkd[row_level(p)]
            rows = pl.ds(f * ROWS + p, 8, SEG)
            oten[rows, :] = value
            oadv[rows, :] = start[f, p] + dt * value
        for number, (source, target) in enumerate(((oadv, adv), (oten, ten))):
            copy = pltpu.make_async_copy(
                source.at[pl.ds(f * ROWS, ROWS)], target.at[f], out_sem.at[number, f])
            copy.start()
            store.append(copy)
    for copy in store:
        copy.wait()


def solution(mesh):
    n_tile, n_lvl = mesh.shape["tile"], mesh.shape["lvl"]
    inner = 8 if n_tile > 8 and n_tile % 8 == 0 else 2
    reach = -(-(n_tile // inner) // 4)
    block, wide = (FIELDS, SEG, 8, CELL), (FIELDS, EXT, 8, CELL)
    flat = (FIELDS * ROWS, CELL)
    most = max((2 * reach + 1) * n_lvl, 3 * inner)
    dma = pltpu.SemaphoreType.DMA
    between = [
        (block, F32), (block, F32), (wide, F32), (wide, F32), ((2, FIELDS, 2, 8, CELL), F32),
        ((8, CELL), F32), ((4, 2 * CELL, CELL), BF16), ((2, 256, CELL), BF16), ((7, 8, CELL), F32),
    ]
    vmem, hbm = pl.BlockSpec(memory_space=pltpu.VMEM), pl.BlockSpec(memory_space=pltpu.HBM)

    def shards(coefficients, level_masks):
        held = pl.pallas_call(
            functools.partial(front, n_tile, n_lvl, inner, reach),
            out_shape=[pltpu.VMEM(shape, dtype) for shape, dtype in between],
            in_specs=[hbm, hbm],
            out_specs=[vmem] * len(between),
            scratch_shapes=[
                pltpu.VMEM(flat, F32), pltpu.SMEM((4, 1, 6), jnp.int32),
                pltpu.VMEM(wide, F32), pltpu.VMEM(wide, F32), pltpu.VMEM((7, 8, CELL), F32),
                pltpu.VMEM((2, 2, 16, CELL), F32), pltpu.VMEM((2, 2, 16, CELL), F32),
                pltpu.VMEM((2, 2, FIELDS, 8, CELL), F32), pltpu.VMEM((2, 2, FIELDS, 8, CELL), F32),
                pltpu.VMEM((2, 1, CELL), F32), pltpu.VMEM((2, most, 1, CELL), F32),
                dma((FIELDS,)), dma(()),
                dma((2, 2)), dma((2, 2)), dma((2, 2)), dma((2, 2)), dma((2,)), dma((2,)),
            ],
            compiler_params=pltpu.CompilerParams(
                collective_id=0, has_side_effects=True, vmem_limit_bytes=57 * 2**20
            ),
        )(coefficients, level_masks)
        result = jax.ShapeDtypeStruct((FIELDS, ROWS, CELL), F32)
        return pl.pallas_call(
            back,
            out_shape=(result, result),
            in_specs=[vmem] * len(between),
            out_specs=(hbm, hbm),
            scratch_shapes=[
                pltpu.VMEM(flat, F32), pltpu.VMEM(flat, F32), pltpu.VMEM(wide, F32),
                pltpu.VMEM(wide, F32), dma((2, FIELDS)),
            ],
            compiler_params=pltpu.CompilerParams(vmem_limit_bytes=24 * 2**20),
        )(*held)

    specs = P(None, "tile", "lvl")
    return jax.shard_map(
        shards, mesh=mesh, in_specs=(specs, P("tile", "lvl", None)), out_specs=(specs, specs),
        check_vma=False,
    )
```

```python
import functools

import jax
import jax.numpy as jnp
from jax import lax
from jax.experimental import pallas as pl
from jax.experimental.pallas import tpu as pltpu
from jax.sharding import PartitionSpec as P

MESH = pl.DeviceIdType.MESH
F32 = jnp.float32
BF16 = jnp.bfloat16
FIELDS = 5
CELL = 128
SEG = 64
PITCH = 72
ROWS = 512
BASE_DENSITY = 1.0
BASE_ENERGY = 2.5
SPACING = 1.0 / CELL


def iota(shape, axis):
    return lax.broadcasted_iota(jnp.int32, shape, axis)


def stride_of(position):
    low = jnp.bitwise_and(position, -position)
    return jnp.where(jnp.bitwise_and(position, 63) == 0, 64, low)


def level_of(stride):
    level = jnp.zeros_like(stride)
    for number in range(1, 7):
        level = jnp.where(stride == 64 >> number, number, level)
    return level


def synthesis_t():
    q, p = iota((CELL, CELL), 0), iota((CELL, CELL), 1)
    s = stride_of(q)
    hat = jnp.maximum(1.0 - jnp.abs(p - q).astype(F32) / s.astype(F32), 0.0)
    return jnp.where(jnp.logical_and(q + s == CELL, p >= q), 1.0, hat)


def analysis_t():
    q, p = iota((CELL, CELL), 0), iota((CELL, CELL), 1)
    s = stride_of(p)
    detail = jnp.bitwise_and(p, 63) != 0
    last = p + s == CELL
    left = jnp.where(jnp.logical_and(detail, q == p - s), jnp.where(last, 1.0, 0.5), 0.0)
    right = jnp.where(
        jnp.logical_and(detail, jnp.logical_and(jnp.logical_not(last), q == p + s)), 0.5, 0.0
    )
    return jnp.where(p == q, 1.0, 0.0) - left - right


def slope_matrix(j, i):
    d = j - i
    near = jnp.where(d == 1, 8.0, 0.0) - jnp.where(d == -1, 8.0, 0.0)
    return near + jnp.where(d == -2, 1.0, 0.0) - jnp.where(d == 2, 1.0, 0.0)


def halo_point(slot):
    return jnp.where(slot < 2, slot - 2, slot + 126)


def dot(a, b):
    return lax.dot_general(a, b, (((1,), (0,)), ((), ())), preferred_element_type=F32)


def halves(x):
    high = x.astype(BF16)
    return high, (x - high.astype(F32)).astype(BF16)


def neighbours(nodes, even):
    following = pltpu.roll(nodes[0], 7, 0)
    end = jnp.where(even, following, nodes[-1])[None]
    return end if nodes.shape[0] == 1 else jnp.concatenate([nodes[1:], end], 0)


def row_synthesis(c, even):
    nodes = c[0:1]
    s = SEG // 2
    while s >= 1:
        count = SEG // (2 * s)
        detail = c.reshape(count, 2 * s, 8, CELL)[:, s]
        middle = detail + 0.5 * (nodes + neighbours(nodes, even))
        nodes = jnp.stack([nodes, middle], 1).reshape(2 * count, 8, CELL)
        s //= 2
    return nodes


def row_analysis(u, even):
    pieces = u[0:1]
    s = SEG // 2
    while s >= 1:
        count = SEG // (2 * s)
        both = u.reshape(count, 2, s, 8, CELL)
        left, middle = both[:, 0, 0], both[:, 1, 0]
        detail = middle - 0.5 * (left + neighbours(left, even))
        pieces = jnp.stack([pieces, detail], 1).reshape(2 * count, 8, CELL)
        s //= 2
    return pieces


def row_level(p):
    return 0 if p == 0 else 6 - ((p & -p).bit_length() - 1)


def primitives(q):
    inverse = 1.0 / q[0]
    vx, vy, vz = q[1] * inverse, q[2] * inverse, q[3] * inverse
    xx, yy, zz = q[1] * vx, q[2] * vy, q[3] * vz
    excess = 0.4 * ((q[4] - BASE_ENERGY) - 0.5 * (xx + yy + zz))
    return inverse, vx, vy, xx, yy, excess


def x_flux(q, prim):
    _, vx, _, xx, _, excess = prim
    enthalpy = q[4] + excess + 0.4 * BASE_ENERGY
    return [q[1], xx + excess, q[2] * vx, q[3] * vx, enthalpy * vx]


def y_flux(q, prim):
    _, _, vy, _, yy, excess = prim
    enthalpy = q[4] + excess + 0.4 * BASE_ENERGY
    return [q[2], q[1] * vy, yy + excess, q[3] * vy, enthalpy * vy]


def speed(prim):
    inverse, vx, vy, _, _, excess = prim
    sound = jnp.sqrt(1.4 * (excess + 0.4 * BASE_ENERGY) * inverse)
    return jnp.maximum(jnp.abs(vx), jnp.abs(vy)) + sound


def pack_edges(u, lane):
    def gather(part):
        width = 64
        while part.shape[0] > 1:
            n = part.shape[0] // 2
            chosen = jnp.bitwise_and(lane + 2, width) != 0
            part = jnp.where(chosen, pltpu.roll(part[n:], width, 2), part[:n])
            width //= 2
        return part[0]

    first, second = gather(u[:32]), pltpu.roll(gather(u[32:]), 2, 1)
    upper = jnp.bitwise_and(lane, 3) >= 2
    return jnp.where(upper, first, second), jnp.where(upper, second, first)


CHUNK = 4
EXT = SEG + 4


def flux_pass(state_at, fx, fy, unroll=False):
    def chunk(c, _):
        rows = pl.ds(c * CHUNK, CHUNK)
        q = state_at(rows)
        prim = primitives(q)
        for f, value in enumerate(x_flux(q, prim)):
            fx[f, rows] = value
        for f, value in enumerate(y_flux(q, prim)):
            fy[f, rows] = value
        return 0

    lax.fori_loop(0, EXT // CHUNK, chunk, 0, unroll=unroll)


def analysed(f, edge, fx, fy, wmat, spread, even):
    g = fx[f]
    slope = 8.0 * (g[3:67] - g[1:65]) - (g[4:68] - g[0:64])
    xh, xl = halves(slope.reshape(ROWS, CELL))
    yh, yl = halves(fy[f, 2:66].reshape(ROWS, CELL))
    out = []
    for part in range(2):
        eh, el = halves(jnp.concatenate([edge[part], edge[part]], 0))
        mask = spread[part]
        eh = jnp.concatenate([eh] * 16, 0) * mask
        el = jnp.concatenate([el] * 16, 0) * mask
        rows = slice(part * 256, part * 256 + 256)
        terms = [xh[rows], yh[rows], xl[rows], yl[rows], eh, el]
        out.append(dot(jnp.concatenate(terms, 1), wmat[1 + part]))
    return row_analysis(jnp.concatenate(out, 0).reshape(SEG, 8, CELL), even)


def build_weights(wmat, spread):
    synth = synthesis_t().astype(BF16)
    at = analysis_t().astype(BF16)
    k, i = iota((CELL, CELL), 0), iota((CELL, CELL), 1)
    wmat[0, :CELL], wmat[0, CELL:2 * CELL] = synth, synth
    slope = dot(slope_matrix(k, i).astype(BF16), at).astype(BF16)
    for part, offset in ((0, 2), (1, 0)):
        edge = slope_matrix(halo_point(jnp.bitwise_and(k + offset, 3)), i).astype(BF16)
        edge = dot(edge, at).astype(BF16)
        for number, block in enumerate((at, slope, at, slope, edge, edge)):
            wmat[1 + part, number * CELL:(number + 1) * CELL] = block
    row, col = iota((32 * 8, CELL), 0), iota((32 * 8, CELL), 1)
    for part, offset in ((0, 2), (1, 0)):
        group = jnp.right_shift(jnp.bitwise_and(col + offset, 127), 2)
        spread[part] = jnp.where(group == jnp.right_shift(row, 3), 1.0, 0.0).astype(BF16)


def build_keep(masks, mk, mkd, sub, lane):
    level = level_of(stride_of(lane))
    owner = jnp.right_shift(sub, 1)
    planes = [jnp.ones((8, CELL), F32)]
    for number in range(6):
        plane = jnp.full((8, CELL), masks[0, 0, number], jnp.int32)
        for t in range(1, 4):
            plane = jnp.where(owner == t, masks[t, 0, number], plane)
        planes.append(plane.astype(F32))
    for number in range(7):
        keep = planes[number]
        for other in range(number + 1, 7):
            keep = jnp.where(level == other, planes[other], keep)
        mk[number] = keep
        mkd[number] = keep * (-0.5 / (12.0 * SPACING))


def front(
    n_tile, n_lvl, inner, reach,
    coef, masks,
    start, half0, st, rr, cols, dts, wmat, spread, mkd,
    cin, lvm, fx, fy, mk,
    row_snd, row_rcv, col_snd, col_rcv, mx_snd, mx_rcv,
    in_sem, mask_sem, row_ss, row_rs, col_ss, col_rs, mx_ss, mx_rs,
):
    outer = n_tile // inner
    tile, lvl = lax.axis_index("tile"), lax.axis_index("lvl")
    z, low = tile // inner, tile % inner
    t_right, t_left = lax.rem(tile + 1, n_tile), lax.rem(tile + n_tile - 1, n_tile)
    l_right, l_left = lax.rem(lvl + 1, n_lvl), lax.rem(lvl + n_lvl - 1, n_lvl)

    def there(dz, dlow, dx):
        to = lax.rem(z + dz, outer) * inner + lax.rem(low + dlow, inner)
        return to, lax.rem(lvl + dx, n_lvl)

    around = sorted(range(1, outer), key=lambda d: -min(d, outer - d))
    plane = [(dlow, dx) for dx in range(n_lvl) for dlow in range(inner) if dlow or dx]
    plane.sort(key=lambda d: -abs(min(d[0], inner - d[0])) // 2 - min(d[1], n_lvl - d[1]))
    groups = [
        [there(dz, 0, 0) for dz in around if min(dz, outer - dz) <= reach]
        + [there(0, dlow, dx) for dlow, dx in plane],
        [there(dz, 0, 0) for dz in around],
    ]
    partners = groups[0] + [(t_right, lvl), (t_left, lvl), (tile, l_right), (tile, l_left)]
    barrier = pltpu.get_barrier_semaphore()
    for partner in partners:
        pl.semaphore_signal(barrier, inc=1, device_id=partner, device_id_type=MESH)

    load_masks = pltpu.make_async_copy(masks, lvm, mask_sem)
    load_masks.start()
    for f in range(FIELDS):
        for g in range(8):
            pltpu.make_async_copy(
                coef.at[f, pl.ds(g * SEG, SEG)], cin.at[pl.ds((f * 8 + g) * PITCH, SEG)],
                in_sem.at[f]).start()

    sub, lane = iota((8, CELL), 0), iota((8, CELL), 1)
    even = jnp.bitwise_and(sub, 1) == 0
    upper = jnp.bitwise_and(lane, 3) >= 2
    coarse = jnp.bitwise_and(lane, 63) == 0
    build_weights(wmat, spread)
    load_masks.wait()
    build_keep(lvm, mk, mkd, sub, lane)

    def synthesise(c):
        high, low_part = halves(c.reshape(ROWS, CELL))
        out = dot(jnp.concatenate([high, low_part], 1), wmat[0, :2 * CELL])
        return row_synthesis(out.reshape(SEG, 8, CELL), even)

    def pack(stage, f, u):
        to_right, to_left = pack_edges(u, lane)
        col_snd[stage, 0, f] = to_right
        col_snd[stage, 1, f] = to_left
        for r in range(2):
            row_snd[stage, 0, pl.ds(2 * f + r, 1), :] = u[62 + r, 7:8]
            row_snd[stage, 1, pl.ds(2 * f + r, 1), :] = u[r, 0:1]

    def edge_copies(stage):
        copies = []
        for side, (t_to, l_to) in enumerate(((t_right, l_right), (t_left, l_left))):
            copies.append(pltpu.make_async_remote_copy(
                col_snd.at[stage, side], col_rcv.at[stage, side],
                col_ss.at[stage, side], col_rs.at[stage, side],
                device_id=(tile, l_to), device_id_type=MESH))
            copies.append(pltpu.make_async_remote_copy(
                row_snd.at[stage, side], row_rcv.at[stage, side],
                row_ss.at[stage, side], row_rs.at[stage, side],
                device_id=(t_to, lvl), device_id_type=MESH))
        return copies

    def rounds(number):
        return [
            pltpu.make_async_remote_copy(
                mx_snd.at[number], mx_rcv.at[number, slot], mx_ss.at[number], mx_rs.at[number],
                device_id=partner, device_id_type=MESH)
            for slot, partner in enumerate(groups[number])
        ]

    def take_top(number, top):
        count = len(groups[number])
        whole = mx_rcv.at[number, pl.ds(0, count)]
        pltpu.make_async_copy(whole, whole, mx_rs.at[number]).wait()
        return jnp.maximum(top, jnp.max(mx_rcv[number, 0:count], 0))

    def take_edges(stage, block):
        for f in range(FIELDS):
            for side in range(2):
                for r in range(2):
                    source = block[f, 64 + r] if side == 0 else block[f, 2 + r]
                    beyond = row_rcv[stage, side, pl.ds(2 * f + r, 1), :]
                    rolled = pltpu.roll(source, 1 if side == 0 else 7, 0)
                    here = r if side == 0 else 66 + r
                    block[f, here] = jnp.where(sub == (0 if side == 0 else 7), beyond, rolled)
            from_left, from_right = col_rcv[stage, 0, f], col_rcv[stage, 1, f]
            cols[stage, f, 0] = jnp.where(upper, from_left, from_right)
            cols[stage, f, 1] = jnp.where(upper, from_right, from_left)

    for f in range(FIELDS):
        pltpu.make_async_copy(coef.at[f], cin.at[pl.ds(f * 8 * PITCH, ROWS)], in_sem.at[f]).wait()
        parts = [
            cin[pl.ds(f * 8 * PITCH + p, 8, PITCH), :] * mk[row_level(p)] for p in range(SEG)
        ]
        parts = jnp.stack(parts, 0)
        start[f] = parts
        base = {0: BASE_DENSITY, 4: BASE_ENERGY}.get(f)
        if base:
            first = jnp.where(coarse, parts[0:1] - base, parts[0:1])
            parts = jnp.concatenate([first, parts[1:]], 0)
        u = synthesise(parts)
        if base:
            u = u + base
        st[f, 2:66] = u

    def fastest(c, top):
        rows = pl.ds(c * CHUNK + 2, CHUNK)
        prim = primitives([st[f, rows] for f in range(FIELDS)])
        return jnp.maximum(top, jnp.max(speed(prim), 0))

    top = lax.fori_loop(0, SEG // CHUNK, fastest, jnp.zeros((8, CELL), F32))
    top = jnp.max(top, 0, keepdims=True)
    mx_snd[0] = top
    pl.semaphore_wait(barrier, len(partners))
    first_round, second_round = rounds(0), rounds(1)
    edges = [edge_copies(0), edge_copies(1)]
    for copy in first_round:
        copy.start()
    for f in range(FIELDS):
        pack(0, f, st[f, 2:66])
    for copy in edges[0]:
        copy.start()

    for copy in edges[0]:
        copy.wait_recv()
    top = take_top(0, top)
    mx_snd[1] = top
    for copy in second_round:
        copy.start()
    take_edges(0, st)
    flux_pass(lambda rows: [st[f, rows] for f in range(FIELDS)], fx, fy)
    q = [cols[0, f] for f in range(FIELDS)]
    edge = y_flux(q, primitives(q))
    for f in range(FIELDS):
        d = analysed(f, edge[f], fx, fy, wmat, spread, even)
        half = jnp.stack([d[p] * mkd[row_level(p)] for p in range(SEG)], 0)
        half0[f] = half
        u = synthesise(half + half)
        rr[f, 2:66] = u
        pack(1, f, u)
    for copy in edges[1]:
        copy.start()
    for copy in edges[1]:
        copy.wait_recv()
    take_edges(1, rr)
    for copy in edges[0] + edges[1] + first_round:
        copy.wait_send()
    top = take_top(1, top)
    top = jnp.max(top, 1, keepdims=True)
    dts[...] = 0.5 * SPACING / jnp.broadcast_to(top, (8, CELL))
    for copy in second_round:
        copy.wait_send()


def back(
    start, half0, st, rr, cols, dts, wmat, spread, mkd, adv, ten, oadv, oten, fx, fy, out_sem
):
    even = jnp.bitwise_and(iota((8, CELL), 0), 1) == 0
    dt = dts[...]
    flux_pass(lambda rows: [st[f, rows] + dt * rr[f, rows] for f in range(FIELDS)], fx, fy, True)
    q = [cols[0, f] + dt * cols[1, f] for f in range(FIELDS)]
    edge = y_flux(q, primitives(q))
    results = ((oadv, adv), (oten, ten))
    for f in range(FIELDS):
        d = analysed(f, edge[f], fx, fy, wmat, spread, even)
        for p in range(SEG):
            value = half0[f, p] + d[p] * mkd[row_level(p)]
            rows = pl.ds(f * 8 * PITCH + p, 8, PITCH)
            oten[rows, :] = value
            oadv[rows, :] = start[f, p] + dt * value
        for number, (source, target) in enumerate(results):
            for g in range(8):
                pltpu.make_async_copy(
                    source.at[pl.ds((f * 8 + g) * PITCH, SEG)], target.at[f, pl.ds(g * SEG, SEG)],
                    out_sem.at[number, f]).start()
    for f in range(FIELDS):
        for number, (source, target) in enumerate(results):
            pltpu.make_async_copy(
                source.at[pl.ds(f * 8 * PITCH, ROWS)], target.at[f], out_sem.at[number, f]).wait()


def solution(mesh):
    n_tile, n_lvl = mesh.shape["tile"], mesh.shape["lvl"]
    inner = 8 if n_tile > 8 and n_tile % 8 == 0 else 2
    reach = -(-(n_tile // inner) // 4)
    block, wide = (FIELDS, SEG, 8, CELL), (FIELDS, EXT, 8, CELL)
    flat = (FIELDS * 8 * PITCH, CELL)
    most = max(inner * n_lvl + 2 * reach, n_tile // inner)
    dma = pltpu.SemaphoreType.DMA
    between = [
        (block, F32), (block, F32), (wide, F32), (wide, F32), ((2, FIELDS, 2, 8, CELL), F32),
        ((8, CELL), F32), ((3, 6 * CELL, CELL), BF16), ((2, 256, CELL), BF16),
        ((7, 8, CELL), F32),
    ]
    vmem, hbm = pl.BlockSpec(memory_space=pltpu.VMEM), pl.BlockSpec(memory_space=pltpu.HBM)

    def shards(coefficients, level_masks):
        held = pl.pallas_call(
            functools.partial(front, n_tile, n_lvl, inner, reach),
            out_shape=[pltpu.VMEM(shape, dtype) for shape, dtype in between],
            in_specs=[hbm, hbm],
            out_specs=[vmem] * len(between),
            scratch_shapes=[
                pltpu.VMEM(flat, F32), pltpu.SMEM((4, 1, 6), jnp.int32),
                pltpu.VMEM(wide, F32), pltpu.VMEM(wide, F32), pltpu.VMEM((7, 8, CELL), F32),
                pltpu.VMEM((2, 2, 16, CELL), F32), pltpu.VMEM((2, 2, 16, CELL), F32),
                pltpu.VMEM((2, 2, FIELDS, 8, CELL), F32), pltpu.VMEM((2, 2, FIELDS, 8, CELL), F32),
                pltpu.VMEM((2, 1, CELL), F32), pltpu.VMEM((2, most, 1, CELL), F32),
                dma((FIELDS,)), dma(()),
                dma((2, 2)), dma((2, 2)), dma((2, 2)), dma((2, 2)), dma((2,)), dma((2,)),
            ],
            compiler_params=pltpu.CompilerParams(
                collective_id=0, has_side_effects=True, vmem_limit_bytes=57 * 2**20
            ),
        )(coefficients, level_masks)
        result = jax.ShapeDtypeStruct((FIELDS, ROWS, CELL), F32)
        return pl.pallas_call(
            back,
            out_shape=(result, result),
            in_specs=[vmem] * len(between),
            out_specs=(hbm, hbm),
            scratch_shapes=[
                pltpu.VMEM(flat, F32), pltpu.VMEM(flat, F32), pltpu.VMEM(wide, F32),
                pltpu.VMEM(wide, F32), dma((2, FIELDS)),
            ],
            compiler_params=pltpu.CompilerParams(vmem_limit_bytes=24 * 2**20),
        )(*held)

    specs = P(None, "tile", "lvl")
    return jax.shard_map(
        shards, mesh=mesh, in_specs=(specs, P("tile", "lvl", None)), out_specs=(specs, specs),
        check_vma=False,
    )
```

```python
import functools

import jax
import jax.numpy as jnp
from jax import lax
from jax.experimental import pallas as pl
from jax.experimental.pallas import tpu as pltpu
from jax.sharding import PartitionSpec as P

MESH = pl.DeviceIdType.MESH
F32 = jnp.float32
BF16 = jnp.bfloat16
FIELDS = 5
CELL = 128
SEG = 64
PITCH = 72
ROWS = 512
BASE_DENSITY = 1.0
BASE_ENERGY = 2.5
SPACING = 1.0 / CELL


def iota(shape, axis):
    return lax.broadcasted_iota(jnp.int32, shape, axis)


def stride_of(position):
    low = jnp.bitwise_and(position, -position)
    return jnp.where(jnp.bitwise_and(position, 63) == 0, 64, low)


def level_of(stride):
    level = jnp.zeros_like(stride)
    for number in range(1, 7):
        level = jnp.where(stride == 64 >> number, number, level)
    return level


def synthesis_t():
    q, p = iota((CELL, CELL), 0), iota((CELL, CELL), 1)
    s = stride_of(q)
    hat = jnp.maximum(1.0 - jnp.abs(p - q).astype(F32) / s.astype(F32), 0.0)
    return jnp.where(jnp.logical_and(q + s == CELL, p >= q), 1.0, hat)


def analysis_t():
    q, p = iota((CELL, CELL), 0), iota((CELL, CELL), 1)
    s = stride_of(p)
    detail = jnp.bitwise_and(p, 63) != 0
    last = p + s == CELL
    left = jnp.where(jnp.logical_and(detail, q == p - s), jnp.where(last, 1.0, 0.5), 0.0)
    right = jnp.where(
        jnp.logical_and(detail, jnp.logical_and(jnp.logical_not(last), q == p + s)), 0.5, 0.0
    )
    return jnp.where(p == q, 1.0, 0.0) - left - right


def slope_matrix(j, i):
    d = j - i
    near = jnp.where(d == 1, 8.0, 0.0) - jnp.where(d == -1, 8.0, 0.0)
    return near + jnp.where(d == -2, 1.0, 0.0) - jnp.where(d == 2, 1.0, 0.0)


def halo_point(slot):
    return jnp.where(slot < 2, slot - 2, slot + 126)


def dot(a, b):
    return lax.dot_general(a, b, (((1,), (0,)), ((), ())), preferred_element_type=F32)


def halves(x):
    high = x.astype(BF16)
    return high, (x - high.astype(F32)).astype(BF16)


def neighbours(nodes, even):
    following = pltpu.roll(nodes[0], 7, 0)
    end = jnp.where(even, following, nodes[-1])[None]
    return end if nodes.shape[0] == 1 else jnp.concatenate([nodes[1:], end], 0)


def row_synthesis(c, even):
    nodes = c[0:1]
    s = SEG // 2
    while s >= 1:
        count = SEG // (2 * s)
        detail = c.reshape(count, 2 * s, 8, CELL)[:, s]
        middle = detail + 0.5 * (nodes + neighbours(nodes, even))
        nodes = jnp.stack([nodes, middle], 1).reshape(2 * count, 8, CELL)
        s //= 2
    return nodes


def row_analysis(u, even):
    pieces = u[0:1]
    s = SEG // 2
    while s >= 1:
        count = SEG // (2 * s)
        both = u.reshape(count, 2, s, 8, CELL)
        left, middle = both[:, 0, 0], both[:, 1, 0]
        detail = middle - 0.5 * (left + neighbours(left, even))
        pieces = jnp.stack([pieces, detail], 1).reshape(2 * count, 8, CELL)
        s //= 2
    return pieces


def row_level(p):
    return 0 if p == 0 else 6 - ((p & -p).bit_length() - 1)


def primitives(q):
    inverse = 1.0 / q[0]
    vx, vy, vz = q[1] * inverse, q[2] * inverse, q[3] * inverse
    xx, yy, zz = q[1] * vx, q[2] * vy, q[3] * vz
    excess = 0.4 * ((q[4] - BASE_ENERGY) - 0.5 * (xx + yy + zz))
    return inverse, vx, vy, xx, yy, excess


def x_flux(q, prim):
    _, vx, _, xx, _, excess = prim
    enthalpy = q[4] + excess + 0.4 * BASE_ENERGY
    return [q[1], xx + excess, q[2] * vx, q[3] * vx, enthalpy * vx]


def y_flux(q, prim):
    _, _, vy, _, yy, excess = prim
    enthalpy = q[4] + excess + 0.4 * BASE_ENERGY
    return [q[2], q[1] * vy, yy + excess, q[3] * vy, enthalpy * vy]


def speed(prim):
    inverse, vx, vy, _, _, excess = prim
    sound = jnp.sqrt(1.4 * (excess + 0.4 * BASE_ENERGY) * inverse)
    return jnp.maximum(jnp.abs(vx), jnp.abs(vy)) + sound


def pack_edges(u, lane):
    def gather(part):
        width = 64
        while part.shape[0] > 1:
            n = part.shape[0] // 2
            chosen = jnp.bitwise_and(lane + 2, width) != 0
            part = jnp.where(chosen, pltpu.roll(part[n:], width, 2), part[:n])
            width //= 2
        return part[0]

    first, second = gather(u[:32]), pltpu.roll(gather(u[32:]), 2, 1)
    upper = jnp.bitwise_and(lane, 3) >= 2
    return jnp.where(upper, first, second), jnp.where(upper, second, first)


CHUNK = 4
EXT = SEG + 4


def flux_pass(state_at, fx, fy, unroll=False):
    def chunk(c, _):
        rows = pl.ds(c * CHUNK, CHUNK)
        q = state_at(rows)
        prim = primitives(q)
        for f, value in enumerate(x_flux(q, prim)):
            fx[f, rows] = value
        for f, value in enumerate(y_flux(q, prim)):
            fy[f, rows] = value
        return 0

    lax.fori_loop(0, EXT // CHUNK, chunk, 0, unroll=unroll)


def analysed(f, edge, fx, fy, wmat, spread, even):
    g = fx[f]
    slope = 8.0 * (g[3:67] - g[1:65]) - (g[4:68] - g[0:64])
    xh, xl = halves(slope.reshape(ROWS, CELL))
    yh, yl = halves(fy[f, 2:66].reshape(ROWS, CELL))
    out = []
    for part in range(2):
        eh, el = halves(jnp.concatenate([edge[part], edge[part]], 0))
        mask = spread[part]
        eh = jnp.concatenate([eh] * 16, 0) * mask
        el = jnp.concatenate([el] * 16, 0) * mask
        rows = slice(part * 256, part * 256 + 256)
        terms = [xh[rows], yh[rows], xl[rows], yl[rows], eh, el]
        out.append(dot(jnp.concatenate(terms, 1), wmat[1 + part]))
    return row_analysis(jnp.concatenate(out, 0).reshape(SEG, 8, CELL), even)


def build_weights(wmat, spread):
    synth = synthesis_t().astype(BF16)
    at = analysis_t().astype(BF16)
    k, i = iota((CELL, CELL), 0), iota((CELL, CELL), 1)
    wmat[0, :CELL], wmat[0, CELL:2 * CELL] = synth, synth
    slope = dot(slope_matrix(k, i).astype(BF16), at).astype(BF16)
    for part, offset in ((0, 2), (1, 0)):
        edge = slope_matrix(halo_point(jnp.bitwise_and(k + offset, 3)), i).astype(BF16)
        edge = dot(edge, at).astype(BF16)
        for number, block in enumerate((at, slope, at, slope, edge, edge)):
            wmat[1 + part, number * CELL:(number + 1) * CELL] = block
    row, col = iota((32 * 8, CELL), 0), iota((32 * 8, CELL), 1)
    for part, offset in ((0, 2), (1, 0)):
        group = jnp.right_shift(jnp.bitwise_and(col + offset, 127), 2)
        spread[part] = jnp.where(group == jnp.right_shift(row, 3), 1.0, 0.0).astype(BF16)


def build_keep(masks, mk, mkd, sub, lane):
    level = level_of(stride_of(lane))
    owner = jnp.right_shift(sub, 1)
    planes = [jnp.ones((8, CELL), F32)]
    for number in range(6):
        plane = jnp.full((8, CELL), masks[0, 0, number], jnp.int32)
        for t in range(1, 4):
            plane = jnp.where(owner == t, masks[t, 0, number], plane)
        planes.append(plane.astype(F32))
    for number in range(7):
        keep = planes[number]
        for other in range(number + 1, 7):
            keep = jnp.where(level == other, planes[other], keep)
        mk[number] = keep
        mkd[number] = keep * (-0.5 / (12.0 * SPACING))


def front(
    n_tile, n_lvl, inner, reach,
    coef, masks,
    start, half0, st, rr, cols, dts, wmat, spread, mkd,
    cin, lvm, fx, fy, mk,
    row_snd, row_rcv, col_snd, col_rcv, mx_snd, mx_rcv,
    in_sem, mask_sem, row_ss, row_rs, col_ss, col_rs, mx_ss, mx_rs,
):
    outer = n_tile // inner
    tile, lvl = lax.axis_index("tile"), lax.axis_index("lvl")
    z, low = tile // inner, tile % inner
    t_right, t_left = lax.rem(tile + 1, n_tile), lax.rem(tile + n_tile - 1, n_tile)
    l_right, l_left = lax.rem(lvl + 1, n_lvl), lax.rem(lvl + n_lvl - 1, n_lvl)

    def there(dz, dlow, dx):
        to = lax.rem(z + dz, outer) * inner + lax.rem(low + dlow, inner)
        return to, lax.rem(lvl + dx, n_lvl)

    around = sorted(range(1, outer), key=lambda d: -min(d, outer - d))
    plane = [(dlow, dx) for dx in range(n_lvl) for dlow in range(inner) if dlow or dx]
    plane.sort(key=lambda d: -abs(min(d[0], inner - d[0])) // 2 - min(d[1], n_lvl - d[1]))
    groups = [
        [there(dz, 0, 0) for dz in around if min(dz, outer - dz) <= reach]
        + [there(0, dlow, dx) for dlow, dx in plane],
        [there(dz, 0, 0) for dz in around],
    ]
    partners = groups[0] + [(t_right, lvl), (t_left, lvl), (tile, l_right), (tile, l_left)]
    barrier = pltpu.get_barrier_semaphore()
    load_masks = pltpu.make_async_copy(masks, lvm, mask_sem)
    load_masks.start()
    for f in range(FIELDS):
        for g in range(8):
            pltpu.make_async_copy(
                coef.at[f, pl.ds(g * SEG, SEG)], cin.at[pl.ds((f * 8 + g) * PITCH, SEG)],
                in_sem.at[f]).start()

    for partner in partners:
        pl.semaphore_signal(barrier, inc=1, device_id=partner, device_id_type=MESH)

    sub, lane = iota((8, CELL), 0), iota((8, CELL), 1)
    even = jnp.bitwise_and(sub, 1) == 0
    upper = jnp.bitwise_and(lane, 3) >= 2
    coarse = jnp.bitwise_and(lane, 63) == 0
    build_weights(wmat, spread)
    load_masks.wait()
    build_keep(lvm, mk, mkd, sub, lane)

    def synthesise(c):
        high, low_part = halves(c.reshape(ROWS, CELL))
        out = dot(jnp.concatenate([high, low_part], 1), wmat[0, :2 * CELL])
        return row_synthesis(out.reshape(SEG, 8, CELL), even)

    def pack(stage, f, u):
        to_right, to_left = pack_edges(u, lane)
        col_snd[stage, 0, f] = to_right
        col_snd[stage, 1, f] = to_left
        for r in range(2):
            row_snd[stage, 0, pl.ds(2 * f + r, 1), :] = u[62 + r, 7:8]
            row_snd[stage, 1, pl.ds(2 * f + r, 1), :] = u[r, 0:1]

    def edge_copies(stage):
        copies = []
        for side, (t_to, l_to) in enumerate(((t_right, l_right), (t_left, l_left))):
            copies.append(pltpu.make_async_remote_copy(
                col_snd.at[stage, side], col_rcv.at[stage, side],
                col_ss.at[stage, side], col_rs.at[stage, side],
                device_id=(tile, l_to), device_id_type=MESH))
            copies.append(pltpu.make_async_remote_copy(
                row_snd.at[stage, side], row_rcv.at[stage, side],
                row_ss.at[stage, side], row_rs.at[stage, side],
                device_id=(t_to, lvl), device_id_type=MESH))
        return copies

    def rounds(number):
        return [
            pltpu.make_async_remote_copy(
                mx_snd.at[number], mx_rcv.at[number, slot], mx_ss.at[number], mx_rs.at[number],
                device_id=partner, device_id_type=MESH)
            for slot, partner in enumerate(groups[number])
        ]

    def take_top(number, top):
        count = len(groups[number])
        whole = mx_rcv.at[number, pl.ds(0, count)]
        pltpu.make_async_copy(whole, whole, mx_rs.at[number]).wait()
        return jnp.maximum(top, jnp.max(mx_rcv[number, 0:count], 0))

    def take_edges(stage, block):
        for f in range(FIELDS):
            for side in range(2):
                for r in range(2):
                    source = block[f, 64 + r] if side == 0 else block[f, 2 + r]
                    beyond = row_rcv[stage, side, pl.ds(2 * f + r, 1), :]
                    rolled = pltpu.roll(source, 1 if side == 0 else 7, 0)
                    here = r if side == 0 else 66 + r
                    block[f, here] = jnp.where(sub == (0 if side == 0 else 7), beyond, rolled)
            from_left, from_right = col_rcv[stage, 0, f], col_rcv[stage, 1, f]
            cols[stage, f, 0] = jnp.where(upper, from_left, from_right)
            cols[stage, f, 1] = jnp.where(upper, from_right, from_left)

    for f in range(FIELDS):
        pltpu.make_async_copy(coef.at[f], cin.at[pl.ds(f * 8 * PITCH, ROWS)], in_sem.at[f]).wait()
        parts = [
            cin[pl.ds(f * 8 * PITCH + p, 8, PITCH), :] * mk[row_level(p)] for p in range(SEG)
        ]
        parts = jnp.stack(parts, 0)
        start[f] = parts
        base = {0: BASE_DENSITY, 4: BASE_ENERGY}.get(f)
        if base:
            first = jnp.where(coarse, parts[0:1] - base, parts[0:1])
            parts = jnp.concatenate([first, parts[1:]], 0)
        u = synthesise(parts)
        if base:
            u = u + base
        st[f, 2:66] = u

    def fastest(c, top):
        rows = pl.ds(c * CHUNK + 2, CHUNK)
        prim = primitives([st[f, rows] for f in range(FIELDS)])
        return jnp.maximum(top, jnp.max(speed(prim), 0))

    top = lax.fori_loop(0, SEG // CHUNK, fastest, jnp.zeros((8, CELL), F32), unroll=True)
    top = jnp.max(top, 0, keepdims=True)
    mx_snd[0] = top
    pl.semaphore_wait(barrier, len(partners))
    first_round, second_round = rounds(0), rounds(1)
    edges = [edge_copies(0), edge_copies(1)]
    for copy in first_round:
        copy.start()
    for f in range(FIELDS):
        pack(0, f, st[f, 2:66])
    for copy in edges[0]:
        copy.start()

    for copy in edges[0]:
        copy.wait_recv()
    top = take_top(0, top)
    mx_snd[1] = top
    for copy in second_round:
        copy.start()
    take_edges(0, st)
    flux_pass(lambda rows: [st[f, rows] for f in range(FIELDS)], fx, fy)
    q = [cols[0, f] for f in range(FIELDS)]
    edge = y_flux(q, primitives(q))
    for f in range(FIELDS):
        d = analysed(f, edge[f], fx, fy, wmat, spread, even)
        half = jnp.stack([d[p] * mkd[row_level(p)] for p in range(SEG)], 0)
        half0[f] = half
        u = synthesise(half + half)
        rr[f, 2:66] = u
        pack(1, f, u)
    for copy in edges[1]:
        copy.start()
    for copy in edges[1]:
        copy.wait_recv()
    take_edges(1, rr)
    for copy in edges[0] + edges[1] + first_round:
        copy.wait_send()
    top = take_top(1, top)
    top = jnp.max(top, 1, keepdims=True)
    dts[...] = 0.5 * SPACING / jnp.broadcast_to(top, (8, CELL))
    for copy in second_round:
        copy.wait_send()


def back(
    start, half0, st, rr, cols, dts, wmat, spread, mkd, adv, ten, oadv, oten, fx, fy, out_sem
):
    even = jnp.bitwise_and(iota((8, CELL), 0), 1) == 0
    dt = dts[...]
    flux_pass(lambda rows: [st[f, rows] + dt * rr[f, rows] for f in range(FIELDS)], fx, fy, True)
    q = [cols[0, f] + dt * cols[1, f] for f in range(FIELDS)]
    edge = y_flux(q, primitives(q))
    results = ((oadv, adv), (oten, ten))
    for f in range(FIELDS):
        d = analysed(f, edge[f], fx, fy, wmat, spread, even)
        for p in range(SEG):
            value = half0[f, p] + d[p] * mkd[row_level(p)]
            rows = pl.ds(f * 8 * PITCH + p, 8, PITCH)
            oten[rows, :] = value
            oadv[rows, :] = start[f, p] + dt * value
        for number, (source, target) in enumerate(results):
            for g in range(8):
                pltpu.make_async_copy(
                    source.at[pl.ds((f * 8 + g) * PITCH, SEG)], target.at[f, pl.ds(g * SEG, SEG)],
                    out_sem.at[number, f]).start()
    for f in range(FIELDS):
        for number, (source, target) in enumerate(results):
            pltpu.make_async_copy(
                source.at[pl.ds(f * 8 * PITCH, ROWS)], target.at[f], out_sem.at[number, f]).wait()


def solution(mesh):
    n_tile, n_lvl = mesh.shape["tile"], mesh.shape["lvl"]
    inner = 8 if n_tile > 8 and n_tile % 8 == 0 else 2
    reach = -(-(n_tile // inner) // 4)
    block, wide = (FIELDS, SEG, 8, CELL), (FIELDS, EXT, 8, CELL)
    flat = (FIELDS * 8 * PITCH, CELL)
    most = max(inner * n_lvl + 2 * reach, n_tile // inner)
    dma = pltpu.SemaphoreType.DMA
    between = [
        (block, F32), (block, F32), (wide, F32), (wide, F32), ((2, FIELDS, 2, 8, CELL), F32),
        ((8, CELL), F32), ((3, 6 * CELL, CELL), BF16), ((2, 256, CELL), BF16),
        ((7, 8, CELL), F32),
    ]
    vmem, hbm = pl.BlockSpec(memory_space=pltpu.VMEM), pl.BlockSpec(memory_space=pltpu.HBM)

    def shards(coefficients, level_masks):
        held = pl.pallas_call(
            functools.partial(front, n_tile, n_lvl, inner, reach),
            out_shape=[pltpu.VMEM(shape, dtype) for shape, dtype in between],
            in_specs=[hbm, hbm],
            out_specs=[vmem] * len(between),
            scratch_shapes=[
                pltpu.VMEM(flat, F32), pltpu.SMEM((4, 1, 6), jnp.int32),
                pltpu.VMEM(wide, F32), pltpu.VMEM(wide, F32), pltpu.VMEM((7, 8, CELL), F32),
                pltpu.VMEM((2, 2, 16, CELL), F32), pltpu.VMEM((2, 2, 16, CELL), F32),
                pltpu.VMEM((2, 2, FIELDS, 8, CELL), F32), pltpu.VMEM((2, 2, FIELDS, 8, CELL), F32),
                pltpu.VMEM((2, 1, CELL), F32), pltpu.VMEM((2, most, 1, CELL), F32),
                dma((FIELDS,)), dma(()),
                dma((2, 2)), dma((2, 2)), dma((2, 2)), dma((2, 2)), dma((2,)), dma((2,)),
            ],
            compiler_params=pltpu.CompilerParams(
                collective_id=0, has_side_effects=True, vmem_limit_bytes=57 * 2**20
            ),
        )(coefficients, level_masks)
        result = jax.ShapeDtypeStruct((FIELDS, ROWS, CELL), F32)
        return pl.pallas_call(
            back,
            out_shape=(result, result),
            in_specs=[vmem] * len(between),
            out_specs=(hbm, hbm),
            scratch_shapes=[
                pltpu.VMEM(flat, F32), pltpu.VMEM(flat, F32), pltpu.VMEM(wide, F32),
                pltpu.VMEM(wide, F32), dma((2, FIELDS)),
            ],
            compiler_params=pltpu.CompilerParams(vmem_limit_bytes=24 * 2**20),
        )(*held)

    specs = P(None, "tile", "lvl")
    return jax.shard_map(
        shards, mesh=mesh, in_specs=(specs, P("tile", "lvl", None)), out_specs=(specs, specs),
        check_vma=False,
    )
```

```python
import functools

import jax
import jax.numpy as jnp
from jax import lax
from jax.experimental import pallas as pl
from jax.experimental.pallas import tpu as pltpu
from jax.sharding import PartitionSpec as P

MESH = pl.DeviceIdType.MESH
F32 = jnp.float32
BF16 = jnp.bfloat16
FIELDS = 5
CELL = 128
SEG = 64
PITCH = 72
ROWS = 512
BASE_DENSITY = 1.0
BASE_ENERGY = 2.5
SPACING = 1.0 / CELL


def iota(shape, axis):
    return lax.broadcasted_iota(jnp.int32, shape, axis)


def stride_of(position):
    low = jnp.bitwise_and(position, -position)
    return jnp.where(jnp.bitwise_and(position, 63) == 0, 64, low)


def level_of(stride):
    level = jnp.zeros_like(stride)
    for number in range(1, 7):
        level = jnp.where(stride == 64 >> number, number, level)
    return level


def synthesis_t():
    q, p = iota((CELL, CELL), 0), iota((CELL, CELL), 1)
    s = stride_of(q)
    hat = jnp.maximum(1.0 - jnp.abs(p - q).astype(F32) / s.astype(F32), 0.0)
    return jnp.where(jnp.logical_and(q + s == CELL, p >= q), 1.0, hat)


def analysis_t():
    q, p = iota((CELL, CELL), 0), iota((CELL, CELL), 1)
    s = stride_of(p)
    detail = jnp.bitwise_and(p, 63) != 0
    last = p + s == CELL
    left = jnp.where(jnp.logical_and(detail, q == p - s), jnp.where(last, 1.0, 0.5), 0.0)
    right = jnp.where(
        jnp.logical_and(detail, jnp.logical_and(jnp.logical_not(last), q == p + s)), 0.5, 0.0
    )
    return jnp.where(p == q, 1.0, 0.0) - left - right


def slope_matrix(j, i):
    d = j - i
    near = jnp.where(d == 1, 8.0, 0.0) - jnp.where(d == -1, 8.0, 0.0)
    return near + jnp.where(d == -2, 1.0, 0.0) - jnp.where(d == 2, 1.0, 0.0)


def halo_point(slot):
    return jnp.where(slot < 2, slot - 2, slot + 126)


def dot(a, b):
    return lax.dot_general(a, b, (((1,), (0,)), ((), ())), preferred_element_type=F32)


def halves(x):
    high = x.astype(BF16)
    return high, (x - high.astype(F32)).astype(BF16)


def neighbours(nodes, even):
    following = pltpu.roll(nodes[0], 7, 0)
    end = jnp.where(even, following, nodes[-1])[None]
    return end if nodes.shape[0] == 1 else jnp.concatenate([nodes[1:], end], 0)


def row_synthesis(c, even):
    nodes = c[0:1]
    s = SEG // 2
    while s >= 1:
        count = SEG // (2 * s)
        detail = c.reshape(count, 2 * s, 8, CELL)[:, s]
        middle = detail + 0.5 * (nodes + neighbours(nodes, even))
        nodes = jnp.stack([nodes, middle], 1).reshape(2 * count, 8, CELL)
        s //= 2
    return nodes


def row_analysis(u, even):
    pieces = u[0:1]
    s = SEG // 2
    while s >= 1:
        count = SEG // (2 * s)
        both = u.reshape(count, 2, s, 8, CELL)
        left, middle = both[:, 0, 0], both[:, 1, 0]
        detail = middle - 0.5 * (left + neighbours(left, even))
        pieces = jnp.stack([pieces, detail], 1).reshape(2 * count, 8, CELL)
        s //= 2
    return pieces


def row_level(p):
    return 0 if p == 0 else 6 - ((p & -p).bit_length() - 1)


def primitives(q):
    inverse = 1.0 / q[0]
    vx, vy, vz = q[1] * inverse, q[2] * inverse, q[3] * inverse
    xx, yy, zz = q[1] * vx, q[2] * vy, q[3] * vz
    excess = 0.4 * ((q[4] - BASE_ENERGY) - 0.5 * (xx + yy + zz))
    return inverse, vx, vy, xx, yy, excess


def x_flux(q, prim):
    _, vx, _, xx, _, excess = prim
    enthalpy = q[4] + excess + 0.4 * BASE_ENERGY
    return [q[1], xx + excess, q[2] * vx, q[3] * vx, enthalpy * vx]


def y_flux(q, prim):
    _, _, vy, _, yy, excess = prim
    enthalpy = q[4] + excess + 0.4 * BASE_ENERGY
    return [q[2], q[1] * vy, yy + excess, q[3] * vy, enthalpy * vy]


def speed(prim):
    inverse, vx, vy, _, _, excess = prim
    sound = jnp.sqrt(1.4 * (excess + 0.4 * BASE_ENERGY) * inverse)
    return jnp.maximum(jnp.abs(vx), jnp.abs(vy)) + sound


def pack_edges(u, lane):
    def gather(part):
        width = 64
        while part.shape[0] > 1:
            n = part.shape[0] // 2
            chosen = jnp.bitwise_and(lane + 2, width) != 0
            part = jnp.where(chosen, pltpu.roll(part[n:], width, 2), part[:n])
            width //= 2
        return part[0]

    first, second = gather(u[:32]), pltpu.roll(gather(u[32:]), 2, 1)
    upper = jnp.bitwise_and(lane, 3) >= 2
    return jnp.where(upper, first, second), jnp.where(upper, second, first)


CHUNK = 4
EXT = SEG + 4


def flux_pass(state_at, fx, fy, unroll=False):
    def chunk(c, _):
        rows = pl.ds(c * CHUNK, CHUNK)
        q = state_at(rows)
        prim = primitives(q)
        for f, value in enumerate(x_flux(q, prim)):
            fx[f, rows] = value
        for f, value in enumerate(y_flux(q, prim)):
            fy[f, rows] = value
        return 0

    lax.fori_loop(0, EXT // CHUNK, chunk, 0, unroll=unroll)


def analysed(f, edge, fx, fy, wmat, spread, even):
    g = fx[f]
    slope = 8.0 * (g[3:67] - g[1:65]) - (g[4:68] - g[0:64])
    xh, xl = halves(slope.reshape(ROWS, CELL))
    yh, yl = halves(fy[f, 2:66].reshape(ROWS, CELL))
    out = []
    for part in range(2):
        eh, el = halves(jnp.concatenate([edge[part], edge[part]], 0))
        mask = spread[part]
        eh = jnp.concatenate([eh] * 16, 0) * mask
        el = jnp.concatenate([el] * 16, 0) * mask
        rows = slice(part * 256, part * 256 + 256)
        terms = [xh[rows], yh[rows], xl[rows], yl[rows], eh, el]
        out.append(dot(jnp.concatenate(terms, 1), wmat[1 + part]))
    return row_analysis(jnp.concatenate(out, 0).reshape(SEG, 8, CELL), even)


def build_weights(wmat, spread):
    synth = synthesis_t().astype(BF16)
    at = analysis_t().astype(BF16)
    k, i = iota((CELL, CELL), 0), iota((CELL, CELL), 1)
    wmat[0, :CELL], wmat[0, CELL:2 * CELL] = synth, synth
    slope = dot(slope_matrix(k, i).astype(BF16), at).astype(BF16)
    for part, offset in ((0, 2), (1, 0)):
        edge = slope_matrix(halo_point(jnp.bitwise_and(k + offset, 3)), i).astype(BF16)
        edge = dot(edge, at).astype(BF16)
        for number, block in enumerate((at, slope, at, slope, edge, edge)):
            wmat[1 + part, number * CELL:(number + 1) * CELL] = block
    row, col = iota((32 * 8, CELL), 0), iota((32 * 8, CELL), 1)
    for part, offset in ((0, 2), (1, 0)):
        group = jnp.right_shift(jnp.bitwise_and(col + offset, 127), 2)
        spread[part] = jnp.where(group == jnp.right_shift(row, 3), 1.0, 0.0).astype(BF16)


def build_keep(masks, mk, mkd, sub, lane):
    level = level_of(stride_of(lane))
    owner = jnp.right_shift(sub, 1)
    planes = [jnp.ones((8, CELL), F32)]
    for number in range(6):
        plane = jnp.full((8, CELL), masks[0, 0, number], jnp.int32)
        for t in range(1, 4):
            plane = jnp.where(owner == t, masks[t, 0, number], plane)
        planes.append(plane.astype(F32))
    for number in range(7):
        keep = planes[number]
        for other in range(number + 1, 7):
            keep = jnp.where(level == other, planes[other], keep)
        mk[number] = keep
        mkd[number] = keep * (-0.5 / (12.0 * SPACING))


def front(
    n_tile, n_lvl, inner, reach,
    coef, masks,
    start, half0, st, rr, cols, dts, wmat, spread, mkd,
    cin, lvm, fx, fy, mk,
    row_snd, row_rcv, col_snd, col_rcv, mx_snd, mx_rcv,
    in_sem, mask_sem, row_ss, row_rs, col_ss, col_rs, mx_ss, mx_rs,
):
    outer = n_tile // inner
    tile, lvl = lax.axis_index("tile"), lax.axis_index("lvl")
    z, low = tile // inner, tile % inner
    t_right, t_left = lax.rem(tile + 1, n_tile), lax.rem(tile + n_tile - 1, n_tile)
    l_right, l_left = lax.rem(lvl + 1, n_lvl), lax.rem(lvl + n_lvl - 1, n_lvl)

    def there(dz, dlow, dx):
        to = lax.rem(z + dz, outer) * inner + lax.rem(low + dlow, inner)
        return to, lax.rem(lvl + dx, n_lvl)

    around = sorted(range(1, outer), key=lambda d: -min(d, outer - d))
    plane = [(dlow, dx) for dx in range(n_lvl) for dlow in range(inner) if dlow or dx]
    plane.sort(key=lambda d: -abs(min(d[0], inner - d[0])) // 2 - min(d[1], n_lvl - d[1]))
    groups = [
        [there(dz, 0, 0) for dz in around if min(dz, outer - dz) <= reach]
        + [there(0, dlow, dx) for dlow, dx in plane],
        [there(dz, 0, 0) for dz in around],
    ]
    partners = groups[0] + [(t_right, lvl), (t_left, lvl), (tile, l_right), (tile, l_left)]
    barrier = pltpu.get_barrier_semaphore()
    load_masks = pltpu.make_async_copy(masks, lvm, mask_sem)
    load_masks.start()
    for f in range(FIELDS):
        for g in range(8):
            pltpu.make_async_copy(
                coef.at[f, pl.ds(g * SEG, SEG)], cin.at[pl.ds((f * 8 + g) * PITCH, SEG)],
                in_sem.at[f]).start()

    for partner in partners:
        pl.semaphore_signal(barrier, inc=1, device_id=partner, device_id_type=MESH)

    sub, lane = iota((8, CELL), 0), iota((8, CELL), 1)
    even = jnp.bitwise_and(sub, 1) == 0
    upper = jnp.bitwise_and(lane, 3) >= 2
    coarse = jnp.bitwise_and(lane, 63) == 0
    build_weights(wmat, spread)
    load_masks.wait()
    build_keep(lvm, mk, mkd, sub, lane)

    def synthesise(c):
        high, low_part = halves(c.reshape(ROWS, CELL))
        out = dot(jnp.concatenate([high, low_part], 1), wmat[0, :2 * CELL])
        return row_synthesis(out.reshape(SEG, 8, CELL), even)

    def pack(stage, f, u):
        to_right, to_left = pack_edges(u, lane)
        col_snd[stage, 0, f] = to_right
        col_snd[stage, 1, f] = to_left
        for r in range(2):
            row_snd[stage, 0, pl.ds(2 * f + r, 1), :] = u[62 + r, 7:8]
            row_snd[stage, 1, pl.ds(2 * f + r, 1), :] = u[r, 0:1]

    def edge_copies(stage):
        copies = []
        for side, (t_to, l_to) in enumerate(((t_right, l_right), (t_left, l_left))):
            copies.append(pltpu.make_async_remote_copy(
                col_snd.at[stage, side], col_rcv.at[stage, side],
                col_ss.at[stage, side], col_rs.at[stage, side],
                device_id=(tile, l_to), device_id_type=MESH))
            copies.append(pltpu.make_async_remote_copy(
                row_snd.at[stage, side], row_rcv.at[stage, side],
                row_ss.at[stage, side], row_rs.at[stage, side],
                device_id=(t_to, lvl), device_id_type=MESH))
        return copies

    def rounds(number):
        return [
            pltpu.make_async_remote_copy(
                mx_snd.at[number], mx_rcv.at[number, slot], mx_ss.at[number], mx_rs.at[number],
                device_id=partner, device_id_type=MESH)
            for slot, partner in enumerate(groups[number])
        ]

    def take_top(number, top):
        count = len(groups[number])
        whole = mx_rcv.at[number, pl.ds(0, count)]
        pltpu.make_async_copy(whole, whole, mx_rs.at[number]).wait()
        return jnp.maximum(top, jnp.max(mx_rcv[number, 0:count], 0))

    def take_edges(stage, block):
        for f in range(FIELDS):
            for side in range(2):
                for r in range(2):
                    source = block[f, 64 + r] if side == 0 else block[f, 2 + r]
                    beyond = row_rcv[stage, side, pl.ds(2 * f + r, 1), :]
                    rolled = pltpu.roll(source, 1 if side == 0 else 7, 0)
                    here = r if side == 0 else 66 + r
                    block[f, here] = jnp.where(sub == (0 if side == 0 else 7), beyond, rolled)
            from_left, from_right = col_rcv[stage, 0, f], col_rcv[stage, 1, f]
            cols[stage, f, 0] = jnp.where(upper, from_left, from_right)
            cols[stage, f, 1] = jnp.where(upper, from_right, from_left)

    for f in range(FIELDS):
        pltpu.make_async_copy(coef.at[f], cin.at[pl.ds(f * 8 * PITCH, ROWS)], in_sem.at[f]).wait()
    for f in range(FIELDS):
        parts = [
            cin[pl.ds(f * 8 * PITCH + p, 8, PITCH), :] * mk[row_level(p)] for p in range(SEG)
        ]
        parts = jnp.stack(parts, 0)
        start[f] = parts
        base = {0: BASE_DENSITY, 4: BASE_ENERGY}.get(f)
        if base:
            first = jnp.where(coarse, parts[0:1] - base, parts[0:1])
            parts = jnp.concatenate([first, parts[1:]], 0)
        u = synthesise(parts)
        if base:
            u = u + base
        st[f, 2:66] = u

    def fastest(c, top):
        rows = pl.ds(c * CHUNK + 2, CHUNK)
        prim = primitives([st[f, rows] for f in range(FIELDS)])
        return jnp.maximum(top, jnp.max(speed(prim), 0))

    top = lax.fori_loop(0, SEG // CHUNK, fastest, jnp.zeros((8, CELL), F32), unroll=True)
    top = jnp.max(top, 0, keepdims=True)
    mx_snd[0] = top
    pl.semaphore_wait(barrier, len(partners))
    first_round, second_round = rounds(0), rounds(1)
    edges = [edge_copies(0), edge_copies(1)]
    for copy in first_round:
        copy.start()
    for f in range(FIELDS):
        pack(0, f, st[f, 2:66])
    for copy in edges[0]:
        copy.start()

    for copy in edges[0]:
        copy.wait_recv()
    top = take_top(0, top)
    mx_snd[1] = top
    for copy in second_round:
        copy.start()
    take_edges(0, st)
    flux_pass(lambda rows: [st[f, rows] for f in range(FIELDS)], fx, fy)
    q = [cols[0, f] for f in range(FIELDS)]
    edge = y_flux(q, primitives(q))
    for f in range(FIELDS):
        d = analysed(f, edge[f], fx, fy, wmat, spread, even)
        half = jnp.stack([d[p] * mkd[row_level(p)] for p in range(SEG)], 0)
        half0[f] = half
        u = synthesise(half + half)
        rr[f, 2:66] = u
        pack(1, f, u)
    for copy in edges[1]:
        copy.start()
    for copy in edges[1]:
        copy.wait_recv()
    take_edges(1, rr)
    for copy in edges[0] + edges[1] + first_round + second_round:
        copy.wait_send()
    top = take_top(1, top)
    top = jnp.max(top, 1, keepdims=True)
    dts[...] = 0.5 * SPACING / jnp.broadcast_to(top, (8, CELL))


def back(
    start, half0, st, rr, cols, dts, wmat, spread, mkd, adv, ten, oadv, oten, fx, fy, out_sem
):
    even = jnp.bitwise_and(iota((8, CELL), 0), 1) == 0
    dt = dts[...]
    flux_pass(lambda rows: [st[f, rows] + dt * rr[f, rows] for f in range(FIELDS)], fx, fy, True)
    q = [cols[0, f] + dt * cols[1, f] for f in range(FIELDS)]
    edge = y_flux(q, primitives(q))
    results = ((oadv, adv), (oten, ten))
    for f in range(FIELDS):
        d = analysed(f, edge[f], fx, fy, wmat, spread, even)
        for p in range(SEG):
            value = half0[f, p] + d[p] * mkd[row_level(p)]
            rows = pl.ds(f * 8 * PITCH + p, 8, PITCH)
            oten[rows, :] = value
            oadv[rows, :] = start[f, p] + dt * value
        for number, (source, target) in enumerate(results):
            for g in range(8):
                pltpu.make_async_copy(
                    source.at[pl.ds((f * 8 + g) * PITCH, SEG)], target.at[f, pl.ds(g * SEG, SEG)],
                    out_sem.at[number, f]).start()
    for f in range(FIELDS):
        for number, (source, target) in enumerate(results):
            pltpu.make_async_copy(
                source.at[pl.ds(f * 8 * PITCH, ROWS)], target.at[f], out_sem.at[number, f]).wait()


def solution(mesh):
    n_tile, n_lvl = mesh.shape["tile"], mesh.shape["lvl"]
    inner = 8 if n_tile > 8 and n_tile % 8 == 0 else 2
    reach = -(-(n_tile // inner) // 4)
    block, wide = (FIELDS, SEG, 8, CELL), (FIELDS, EXT, 8, CELL)
    flat = (FIELDS * 8 * PITCH, CELL)
    most = max(inner * n_lvl + 2 * reach, n_tile // inner)
    dma = pltpu.SemaphoreType.DMA
    between = [
        (block, F32), (block, F32), (wide, F32), (wide, F32), ((2, FIELDS, 2, 8, CELL), F32),
        ((8, CELL), F32), ((3, 6 * CELL, CELL), BF16), ((2, 256, CELL), BF16),
        ((7, 8, CELL), F32),
    ]
    vmem, hbm = pl.BlockSpec(memory_space=pltpu.VMEM), pl.BlockSpec(memory_space=pltpu.HBM)

    def shards(coefficients, level_masks):
        held = pl.pallas_call(
            functools.partial(front, n_tile, n_lvl, inner, reach),
            out_shape=[pltpu.VMEM(shape, dtype) for shape, dtype in between],
            in_specs=[hbm, hbm],
            out_specs=[vmem] * len(between),
            scratch_shapes=[
                pltpu.VMEM(flat, F32), pltpu.SMEM((4, 1, 6), jnp.int32),
                pltpu.VMEM(wide, F32), pltpu.VMEM(wide, F32), pltpu.VMEM((7, 8, CELL), F32),
                pltpu.VMEM((2, 2, 16, CELL), F32), pltpu.VMEM((2, 2, 16, CELL), F32),
                pltpu.VMEM((2, 2, FIELDS, 8, CELL), F32), pltpu.VMEM((2, 2, FIELDS, 8, CELL), F32),
                pltpu.VMEM((2, 1, CELL), F32), pltpu.VMEM((2, most, 1, CELL), F32),
                dma((FIELDS,)), dma(()),
                dma((2, 2)), dma((2, 2)), dma((2, 2)), dma((2, 2)), dma((2,)), dma((2,)),
            ],
            compiler_params=pltpu.CompilerParams(
                collective_id=0, has_side_effects=True, vmem_limit_bytes=57 * 2**20
            ),
        )(coefficients, level_masks)
        result = jax.ShapeDtypeStruct((FIELDS, ROWS, CELL), F32)
        return pl.pallas_call(
            back,
            out_shape=(result, result),
            in_specs=[vmem] * len(between),
            out_specs=(hbm, hbm),
            scratch_shapes=[
                pltpu.VMEM(flat, F32), pltpu.VMEM(flat, F32), pltpu.VMEM(wide, F32),
                pltpu.VMEM(wide, F32), dma((2, FIELDS)),
            ],
            compiler_params=pltpu.CompilerParams(vmem_limit_bytes=24 * 2**20),
        )(*held)

    specs = P(None, "tile", "lvl")
    return jax.shard_map(
        shards, mesh=mesh, in_specs=(specs, P("tile", "lvl", None)), out_specs=(specs, specs),
        check_vma=False,
    )
```

```python
import functools

import jax
import jax.numpy as jnp
from jax import lax
from jax.experimental import pallas as pl
from jax.experimental.pallas import tpu as pltpu
from jax.sharding import PartitionSpec as P

MESH = pl.DeviceIdType.MESH
F32 = jnp.float32
BF16 = jnp.bfloat16
FIELDS = 5
CELL = 128
SEG = 64
PITCH = 72
ROWS = 512
BASE_DENSITY = 1.0
BASE_ENERGY = 2.5
SPACING = 1.0 / CELL


def iota(shape, axis):
    return lax.broadcasted_iota(jnp.int32, shape, axis)


def stride_of(position):
    low = jnp.bitwise_and(position, -position)
    return jnp.where(jnp.bitwise_and(position, 63) == 0, 64, low)


def level_of(stride):
    level = jnp.zeros_like(stride)
    for number in range(1, 7):
        level = jnp.where(stride == 64 >> number, number, level)
    return level


def synthesis_t():
    q, p = iota((CELL, CELL), 0), iota((CELL, CELL), 1)
    s = stride_of(q)
    hat = jnp.maximum(1.0 - jnp.abs(p - q).astype(F32) / s.astype(F32), 0.0)
    return jnp.where(jnp.logical_and(q + s == CELL, p >= q), 1.0, hat)


def analysis_t():
    q, p = iota((CELL, CELL), 0), iota((CELL, CELL), 1)
    s = stride_of(p)
    detail = jnp.bitwise_and(p, 63) != 0
    last = p + s == CELL
    left = jnp.where(jnp.logical_and(detail, q == p - s), jnp.where(last, 1.0, 0.5), 0.0)
    right = jnp.where(
        jnp.logical_and(detail, jnp.logical_and(jnp.logical_not(last), q == p + s)), 0.5, 0.0
    )
    return jnp.where(p == q, 1.0, 0.0) - left - right


def slope_matrix(j, i):
    d = j - i
    near = jnp.where(d == 1, 8.0, 0.0) - jnp.where(d == -1, 8.0, 0.0)
    return near + jnp.where(d == -2, 1.0, 0.0) - jnp.where(d == 2, 1.0, 0.0)


def halo_point(slot):
    return jnp.where(slot < 2, slot - 2, slot + 126)


def dot(a, b):
    return lax.dot_general(a, b, (((1,), (0,)), ((), ())), preferred_element_type=F32)


def halves(x):
    high = x.astype(BF16)
    return high, (x - high.astype(F32)).astype(BF16)


def neighbours(nodes, even):
    following = pltpu.roll(nodes[0], 7, 0)
    end = jnp.where(even, following, nodes[-1])[None]
    return end if nodes.shape[0] == 1 else jnp.concatenate([nodes[1:], end], 0)


def row_synthesis(c, even):
    nodes = c[0:1]
    s = SEG // 2
    while s >= 1:
        count = SEG // (2 * s)
        detail = c.reshape(count, 2 * s, 8, CELL)[:, s]
        middle = detail + 0.5 * (nodes + neighbours(nodes, even))
        nodes = jnp.stack([nodes, middle], 1).reshape(2 * count, 8, CELL)
        s //= 2
    return nodes


def row_analysis(u, even):
    pieces = u[0:1]
    s = SEG // 2
    while s >= 1:
        count = SEG // (2 * s)
        both = u.reshape(count, 2, s, 8, CELL)
        left, middle = both[:, 0, 0], both[:, 1, 0]
        detail = middle - 0.5 * (left + neighbours(left, even))
        pieces = jnp.stack([pieces, detail], 1).reshape(2 * count, 8, CELL)
        s //= 2
    return pieces


def row_level(p):
    return 0 if p == 0 else 6 - ((p & -p).bit_length() - 1)


def primitives(q):
    inverse = 1.0 / q[0]
    vx, vy, vz = q[1] * inverse, q[2] * inverse, q[3] * inverse
    xx, yy, zz = q[1] * vx, q[2] * vy, q[3] * vz
    excess = 0.4 * ((q[4] - BASE_ENERGY) - 0.5 * (xx + yy + zz))
    return inverse, vx, vy, xx, yy, excess


def x_flux(q, prim):
    _, vx, _, xx, _, excess = prim
    enthalpy = q[4] + excess + 0.4 * BASE_ENERGY
    return [q[1], xx + excess, q[2] * vx, q[3] * vx, enthalpy * vx]


def y_flux(q, prim):
    _, _, vy, _, yy, excess = prim
    enthalpy = q[4] + excess + 0.4 * BASE_ENERGY
    return [q[2], q[1] * vy, yy + excess, q[3] * vy, enthalpy * vy]


def speed(prim):
    inverse, vx, vy, _, _, excess = prim
    sound = jnp.sqrt(1.4 * (excess + 0.4 * BASE_ENERGY) * inverse)
    return jnp.maximum(jnp.abs(vx), jnp.abs(vy)) + sound


def pack_edges(u, lane):
    def gather(part):
        width = 64
        while part.shape[0] > 1:
            n = part.shape[0] // 2
            chosen = jnp.bitwise_and(lane + 2, width) != 0
            part = jnp.where(chosen, pltpu.roll(part[n:], width, 2), part[:n])
            width //= 2
        return part[0]

    first, second = gather(u[:32]), pltpu.roll(gather(u[32:]), 2, 1)
    upper = jnp.bitwise_and(lane, 3) >= 2
    return jnp.where(upper, first, second), jnp.where(upper, second, first)


CHUNK = 4
EXT = SEG + 4


def flux_pass(state_at, fx, fy, unroll=False):
    def chunk(c, _):
        rows = pl.ds(c * CHUNK, CHUNK)
        q = state_at(rows)
        prim = primitives(q)
        for f, value in enumerate(x_flux(q, prim)):
            fx[f, rows] = value
        for f, value in enumerate(y_flux(q, prim)):
            fy[f, rows] = value
        return 0

    lax.fori_loop(0, EXT // CHUNK, chunk, 0, unroll=unroll)


def analysed(f, edge, fx, fy, wmat, spread, even):
    g = fx[f]
    slope = 8.0 * (g[3:67] - g[1:65]) - (g[4:68] - g[0:64])
    xh, xl = halves(slope.reshape(ROWS, CELL))
    yh, yl = halves(fy[f, 2:66].reshape(ROWS, CELL))
    out = []
    for part in range(2):
        eh, el = halves(jnp.concatenate([edge[part], edge[part]], 0))
        mask = spread[part]
        eh = jnp.concatenate([eh] * 16, 0) * mask
        el = jnp.concatenate([el] * 16, 0) * mask
        rows = slice(part * 256, part * 256 + 256)
        terms = [xh[rows], yh[rows], xl[rows], yl[rows], eh, el]
        out.append(dot(jnp.concatenate(terms, 1), wmat[1 + part]))
    return row_analysis(jnp.concatenate(out, 0).reshape(SEG, 8, CELL), even)


def build_weights(wmat, spread):
    synth = synthesis_t().astype(BF16)
    at = analysis_t().astype(BF16)
    k, i = iota((CELL, CELL), 0), iota((CELL, CELL), 1)
    wmat[0, :CELL], wmat[0, CELL:2 * CELL] = synth, synth
    slope = dot(slope_matrix(k, i).astype(BF16), at).astype(BF16)
    for part, offset in ((0, 2), (1, 0)):
        edge = slope_matrix(halo_point(jnp.bitwise_and(k + offset, 3)), i).astype(BF16)
        edge = dot(edge, at).astype(BF16)
        for number, block in enumerate((at, slope, at, slope, edge, edge)):
            wmat[1 + part, number * CELL:(number + 1) * CELL] = block
    row, col = iota((32 * 8, CELL), 0), iota((32 * 8, CELL), 1)
    for part, offset in ((0, 2), (1, 0)):
        group = jnp.right_shift(jnp.bitwise_and(col + offset, 127), 2)
        spread[part] = jnp.where(group == jnp.right_shift(row, 3), 1.0, 0.0).astype(BF16)


def build_keep(masks, mk, mkd, sub, lane):
    level = level_of(stride_of(lane))
    owner = jnp.right_shift(sub, 1)
    planes = [jnp.ones((8, CELL), F32)]
    for number in range(6):
        plane = jnp.full((8, CELL), masks[0, 0, number], jnp.int32)
        for t in range(1, 4):
            plane = jnp.where(owner == t, masks[t, 0, number], plane)
        planes.append(plane.astype(F32))
    for number in range(7):
        keep = planes[number]
        for other in range(number + 1, 7):
            keep = jnp.where(level == other, planes[other], keep)
        mk[number] = keep
        mkd[number] = keep * (-0.5 / (12.0 * SPACING))


def front(
    n_tile, n_lvl, inner, reach,
    coef, masks,
    start, half0, st, rr, cols, dts, wmat, spread, mkd,
    cin, lvm, fx, fy, mk,
    row_snd, row_rcv, col_snd, col_rcv, mx_snd, mx_rcv,
    in_sem, mask_sem, row_ss, row_rs, col_ss, col_rs, mx_ss, mx_rs,
):
    outer = n_tile // inner
    tile, lvl = lax.axis_index("tile"), lax.axis_index("lvl")
    z, low = tile // inner, tile % inner
    t_right, t_left = lax.rem(tile + 1, n_tile), lax.rem(tile + n_tile - 1, n_tile)
    l_right, l_left = lax.rem(lvl + 1, n_lvl), lax.rem(lvl + n_lvl - 1, n_lvl)

    def there(dz, dlow, dx):
        to = lax.rem(z + dz, outer) * inner + lax.rem(low + dlow, inner)
        return to, lax.rem(lvl + dx, n_lvl)

    around = sorted(range(1, outer), key=lambda d: -min(d, outer - d))
    plane = [(dlow, dx) for dx in range(n_lvl) for dlow in range(inner) if dlow or dx]
    plane.sort(key=lambda d: -abs(min(d[0], inner - d[0])) // 2 - min(d[1], n_lvl - d[1]))
    groups = [
        [there(dz, 0, 0) for dz in around if min(dz, outer - dz) <= reach]
        + [there(0, dlow, dx) for dlow, dx in plane],
        [there(dz, 0, 0) for dz in around],
    ]
    partners = groups[0] + [(t_right, lvl), (t_left, lvl), (tile, l_right), (tile, l_left)]
    barrier = pltpu.get_barrier_semaphore()
    for partner in partners:
        pl.semaphore_signal(barrier, inc=1, device_id=partner, device_id_type=MESH)

    load_masks = pltpu.make_async_copy(masks, lvm, mask_sem)
    load_masks.start()
    for f in range(FIELDS):
        for g in range(8):
            pltpu.make_async_copy(
                coef.at[f, pl.ds(g * SEG, SEG)], cin.at[pl.ds((f * 8 + g) * PITCH, SEG)],
                in_sem.at[f]).start()

    sub, lane = iota((8, CELL), 0), iota((8, CELL), 1)
    even = jnp.bitwise_and(sub, 1) == 0
    upper = jnp.bitwise_and(lane, 3) >= 2
    coarse = jnp.bitwise_and(lane, 63) == 0
    build_weights(wmat, spread)
    load_masks.wait()
    build_keep(lvm, mk, mkd, sub, lane)

    def synthesise(c):
        high, low_part = halves(c.reshape(ROWS, CELL))
        out = dot(jnp.concatenate([high, low_part], 1), wmat[0, :2 * CELL])
        return row_synthesis(out.reshape(SEG, 8, CELL), even)

    def pack(stage, f, u):
        to_right, to_left = pack_edges(u, lane)
        col_snd[stage, 0, f] = to_right
        col_snd[stage, 1, f] = to_left
        for r in range(2):
            row_snd[stage, 0, pl.ds(2 * f + r, 1), :] = u[62 + r, 7:8]
            row_snd[stage, 1, pl.ds(2 * f + r, 1), :] = u[r, 0:1]

    def edge_copies(stage):
        copies = []
        for side, (t_to, l_to) in enumerate(((t_right, l_right), (t_left, l_left))):
            copies.append(pltpu.make_async_remote_copy(
                col_snd.at[stage, side], col_rcv.at[stage, side],
                col_ss.at[stage, side], col_rs.at[stage, side],
                device_id=(tile, l_to), device_id_type=MESH))
            copies.append(pltpu.make_async_remote_copy(
                row_snd.at[stage, side], row_rcv.at[stage, side],
                row_ss.at[stage, side], row_rs.at[stage, side],
                device_id=(t_to, lvl), device_id_type=MESH))
        return copies

    def rounds(number):
        return [
            pltpu.make_async_remote_copy(
                mx_snd.at[number], mx_rcv.at[number, slot], mx_ss.at[number], mx_rs.at[number],
                device_id=partner, device_id_type=MESH)
            for slot, partner in enumerate(groups[number])
        ]

    def take_top(number, top):
        count = len(groups[number])
        whole = mx_rcv.at[number, pl.ds(0, count)]
        pltpu.make_async_copy(whole, whole, mx_rs.at[number]).wait()
        return jnp.maximum(top, jnp.max(mx_rcv[number, 0:count], 0))

    def take_edges(stage, block):
        for f in range(FIELDS):
            for side in range(2):
                for r in range(2):
                    source = block[f, 64 + r] if side == 0 else block[f, 2 + r]
                    beyond = row_rcv[stage, side, pl.ds(2 * f + r, 1), :]
                    rolled = pltpu.roll(source, 1 if side == 0 else 7, 0)
                    here = r if side == 0 else 66 + r
                    block[f, here] = jnp.where(sub == (0 if side == 0 else 7), beyond, rolled)
            from_left, from_right = col_rcv[stage, 0, f], col_rcv[stage, 1, f]
            cols[stage, f, 0] = jnp.where(upper, from_left, from_right)
            cols[stage, f, 1] = jnp.where(upper, from_right, from_left)

    for f in range(FIELDS):
        pltpu.make_async_copy(coef.at[f], cin.at[pl.ds(f * 8 * PITCH, ROWS)], in_sem.at[f]).wait()
    for f in range(FIELDS):
        parts = [
            cin[pl.ds(f * 8 * PITCH + p, 8, PITCH), :] * mk[row_level(p)] for p in range(SEG)
        ]
        parts = jnp.stack(parts, 0)
        start[f] = parts
        base = {0: BASE_DENSITY, 4: BASE_ENERGY}.get(f)
        if base:
            first = jnp.where(coarse, parts[0:1] - base, parts[0:1])
            parts = jnp.concatenate([first, parts[1:]], 0)
        u = synthesise(parts)
        if base:
            u = u + base
        st[f, 2:66] = u

    def fastest(c, top):
        rows = pl.ds(c * CHUNK + 2, CHUNK)
        prim = primitives([st[f, rows] for f in range(FIELDS)])
        return jnp.maximum(top, jnp.max(speed(prim), 0))

    top = lax.fori_loop(0, SEG // CHUNK, fastest, jnp.zeros((8, CELL), F32), unroll=True)
    top = jnp.max(top, 0, keepdims=True)
    mx_snd[0] = top
    pl.semaphore_wait(barrier, len(partners))
    first_round, second_round = rounds(0), rounds(1)
    edges = [edge_copies(0), edge_copies(1)]
    for copy in first_round:
        copy.start()
    for f in range(FIELDS):
        pack(0, f, st[f, 2:66])
    for copy in edges[0]:
        copy.start()

    for copy in edges[0]:
        copy.wait_recv()
    top = take_top(0, top)
    mx_snd[1] = top
    for copy in second_round:
        copy.start()
    take_edges(0, st)
    flux_pass(lambda rows: [st[f, rows] for f in range(FIELDS)], fx, fy)
    q = [cols[0, f] for f in range(FIELDS)]
    edge = y_flux(q, primitives(q))
    for f in range(FIELDS):
        d = analysed(f, edge[f], fx, fy, wmat, spread, even)
        half = jnp.stack([d[p] * mkd[row_level(p)] for p in range(SEG)], 0)
        half0[f] = half
        u = synthesise(half + half)
        rr[f, 2:66] = u
        pack(1, f, u)
    for copy in edges[1]:
        copy.start()
    for copy in edges[1]:
        copy.wait_recv()
    take_edges(1, rr)
    for copy in edges[0] + edges[1] + first_round:
        copy.wait_send()
    top = take_top(1, top)
    top = jnp.max(top, 1, keepdims=True)
    dts[...] = 0.5 * SPACING / jnp.broadcast_to(top, (8, CELL))
    for copy in second_round:
        copy.wait_send()


def back(
    start, half0, st, rr, cols, dts, wmat, spread, mkd, adv, ten, oadv, oten, fx, fy, out_sem
):
    even = jnp.bitwise_and(iota((8, CELL), 0), 1) == 0
    dt = dts[...]
    flux_pass(lambda rows: [st[f, rows] + dt * rr[f, rows] for f in range(FIELDS)], fx, fy, True)
    q = [cols[0, f] + dt * cols[1, f] for f in range(FIELDS)]
    edge = y_flux(q, primitives(q))
    results = ((oadv, adv), (oten, ten))
    for f in range(FIELDS):
        d = analysed(f, edge[f], fx, fy, wmat, spread, even)
        for p in range(SEG):
            value = half0[f, p] + d[p] * mkd[row_level(p)]
            rows = pl.ds(f * 8 * PITCH + p, 8, PITCH)
            oten[rows, :] = value
            oadv[rows, :] = start[f, p] + dt * value
        for number, (source, target) in enumerate(results):
            for g in range(8):
                pltpu.make_async_copy(
                    source.at[pl.ds((f * 8 + g) * PITCH, SEG)], target.at[f, pl.ds(g * SEG, SEG)],
                    out_sem.at[number, f]).start()
    for f in range(FIELDS):
        for number, (source, target) in enumerate(results):
            pltpu.make_async_copy(
                source.at[pl.ds(f * 8 * PITCH, ROWS)], target.at[f], out_sem.at[number, f]).wait()


def solution(mesh):
    n_tile, n_lvl = mesh.shape["tile"], mesh.shape["lvl"]
    inner = 8 if n_tile > 8 and n_tile % 8 == 0 else 2
    reach = -(-(n_tile // inner) // 4)
    block, wide = (FIELDS, SEG, 8, CELL), (FIELDS, EXT, 8, CELL)
    flat = (FIELDS * 8 * PITCH, CELL)
    most = max(inner * n_lvl + 2 * reach, n_tile // inner)
    dma = pltpu.SemaphoreType.DMA
    between = [
        (block, F32), (block, F32), (wide, F32), (wide, F32), ((2, FIELDS, 2, 8, CELL), F32),
        ((8, CELL), F32), ((3, 6 * CELL, CELL), BF16), ((2, 256, CELL), BF16),
        ((7, 8, CELL), F32),
    ]
    vmem, hbm = pl.BlockSpec(memory_space=pltpu.VMEM), pl.BlockSpec(memory_space=pltpu.HBM)

    def shards(coefficients, level_masks):
        held = pl.pallas_call(
            functools.partial(front, n_tile, n_lvl, inner, reach),
            out_shape=[pltpu.VMEM(shape, dtype) for shape, dtype in between],
            in_specs=[hbm, hbm],
            out_specs=[vmem] * len(between),
            scratch_shapes=[
                pltpu.VMEM(flat, F32), pltpu.SMEM((4, 1, 6), jnp.int32),
                pltpu.VMEM(wide, F32), pltpu.VMEM(wide, F32), pltpu.VMEM((7, 8, CELL), F32),
                pltpu.VMEM((2, 2, 16, CELL), F32), pltpu.VMEM((2, 2, 16, CELL), F32),
                pltpu.VMEM((2, 2, FIELDS, 8, CELL), F32), pltpu.VMEM((2, 2, FIELDS, 8, CELL), F32),
                pltpu.VMEM((2, 1, CELL), F32), pltpu.VMEM((2, most, 1, CELL), F32),
                dma((FIELDS,)), dma(()),
                dma((2, 2)), dma((2, 2)), dma((2, 2)), dma((2, 2)), dma((2,)), dma((2,)),
            ],
            compiler_params=pltpu.CompilerParams(
                collective_id=0, has_side_effects=True, vmem_limit_bytes=57 * 2**20
            ),
        )(coefficients, level_masks)
        result = jax.ShapeDtypeStruct((FIELDS, ROWS, CELL), F32)
        return pl.pallas_call(
            back,
            out_shape=(result, result),
            in_specs=[vmem] * len(between),
            out_specs=(hbm, hbm),
            scratch_shapes=[
                pltpu.VMEM(flat, F32), pltpu.VMEM(flat, F32), pltpu.VMEM(wide, F32),
                pltpu.VMEM(wide, F32), dma((2, FIELDS)),
            ],
            compiler_params=pltpu.CompilerParams(vmem_limit_bytes=24 * 2**20),
        )(*held)

    specs = P(None, "tile", "lvl")
    return jax.shard_map(
        shards, mesh=mesh, in_specs=(specs, P("tile", "lvl", None)), out_specs=(specs, specs),
        check_vma=False,
    )
```
